128 devices in a mesh: row: 8 (over x, core), col: 16 (over z, y).
Axes of the slice: x: 4, y: 4, z: 4, core: 2. Of those that a mesh axis runs over, the one named last changes fastest.
Arguments:
- tile_list: int32 [2048, 2], P(('row', 'col')), may hold values from -1 to 255, as said below
- tile_values: bfloat16 [2048, 512, 512], P(('row', 'col'))
- block_order: int32 [256], replicated, may hold values from 0 to 255, as said below
- basis: bfloat16 [256, 512, 256], P(('row', 'col')), may hold values from -8 to 8
Outputs:
- basis_out: bfloat16 [256, 512, 256], P(('row', 'col'))
- projected: float32 [256, 256], replicated
The draws below stay inside these ranges and needn't reach their ends.
Inputs may be any that keep to these rules, and one draw needn't show every extreme that they name: `block_order`: A permutation of the channel blocks; slot p lies on device p // 2 in row-major order of (row, col). `tile_list`: slots of device (i, j) hold tiles whose row block sits in a slot of a device of row index i and whose column block sits in a slot of a device of column index j; each unordered pair of blocks appears at most once in all; empty slots hold -1 in both columns and may stand anywhere among a device's slots; every device holds at most 16 tiles and some device holds exactly 16.
All inputs are finite; a program needn't handle non-finite values.
Results may differ from the reference program's by a relative error of at most 0.0017.
Values may be sent and summed in bfloat16 or wider, within the bound.
No kernel may reach another device: no remote copies, remote signals or barrier semaphores. Data moves between devices by JAX's collectives and lax.ppermute only.
A program may use at most 128 MiB of HBM per device.

```python
import jax
import jax.numpy as jnp
from jax import lax

B = 512
K = 256
BLK_DEV = 2
TPD = 16
ROW_GROUP = 32
COL_GROUP = 16
NB = 256
N = 131072
SLOTS = 2048


def make_plan(key):
    base = jax.random.fold_in(key, 9173)
    order_key, score_key, count_key = jax.random.split(base, 3)
    order = jax.random.permutation(order_key, NB).astype(jnp.int32)
    col_count = ROW_GROUP // BLK_DEV
    device_count = NB // BLK_DEV
    devices = jnp.arange(device_count, dtype=jnp.int32)
    row_index = devices // col_count
    col_index = devices % col_count
    row_slots = row_index[:, None] * ROW_GROUP + jnp.arange(ROW_GROUP, dtype=jnp.int32)[None, :]
    group_pos = jnp.arange(COL_GROUP, dtype=jnp.int32)
    col_slots = ((group_pos // BLK_DEV)[None, :] * col_count + col_index[:, None]) * BLK_DEV + (group_pos % BLK_DEV)[None, :]
    first_block = jnp.broadcast_to(order[row_slots][:, :, None], (device_count, ROW_GROUP, COL_GROUP))
    second_block = jnp.broadcast_to(order[col_slots][:, None, :], (device_count, ROW_GROUP, COL_GROUP))
    odd_sum = (first_block + second_block) % 2 == 1
    canon = (first_block == second_block) | ((first_block < second_block) != odd_sum)
    cand = ROW_GROUP * COL_GROUP
    canon = canon.reshape(device_count, cand)
    first_flat = first_block.reshape(device_count, cand)
    second_flat = second_block.reshape(device_count, cand)
    index_row = jnp.arange(cand, dtype=jnp.int32)[None, :]
    noise = jax.random.randint(score_key, (device_count, cand), 0, 65536, dtype=jnp.int32)
    score = jnp.where(canon, noise * cand + index_row, -1 - index_row)
    _, picked = lax.top_k(score, TPD)
    canon_count = jnp.sum(canon.astype(jnp.int32), axis=1)
    counts = jax.random.randint(count_key, (device_count,), TPD // 4, TPD + 1, dtype=jnp.int32)
    fullest = jnp.argmax(canon_count)
    counts = counts.at[fullest].set(TPD)
    counts = jnp.minimum(counts, canon_count)
    live = jnp.arange(TPD, dtype=jnp.int32)[None, :] < counts[:, None]
    first_pick = jnp.take_along_axis(first_flat, picked, axis=1)
    second_pick = jnp.take_along_axis(second_flat, picked, axis=1)
    tiles = jnp.stack([jnp.where(live, first_pick, -1), jnp.where(live, second_pick, -1)], axis=-1)
    return (order, tiles.reshape(SLOTS, 2).astype(jnp.int32))


def draw_block_order(key, part):
    order, _ = make_plan(key)
    return order


def draw_tile_list(key, part):
    _, tiles = make_plan(key)
    return tiles


def draw_tile_values(key, part):
    value_key = jax.random.fold_in(key, 4421)
    sigma = (B * TPD / BLK_DEV) ** (-0.5)
    values = jax.random.normal(value_key, (SLOTS, B, B), jnp.float32) * sigma
    return values.astype(jnp.bfloat16)


def draw_basis(key, part):
    basis_key = jax.random.fold_in(key, 6607)
    leading_key, partner_key, column_key = jax.random.split(basis_key, 3)
    half_rank = K // 2
    ladder = jnp.arange(half_rank, dtype=jnp.float32) / (half_rank - 1)
    offsets = 0.004 * jnp.exp(ladder * 4.317488)
    leading = jnp.clip(jax.random.normal(leading_key, (NB, B, half_rank), jnp.float32), -5.0, 5.0)
    partner_noise = jnp.clip(jax.random.normal(partner_key, (NB, B, half_rank), jnp.float32), -5.0, 5.0)
    partner = leading + offsets * partner_noise
    paired = jnp.stack([leading, partner], axis=3).reshape(NB, B, K)
    column_order = jax.random.permutation(column_key, K).astype(jnp.int32)
    return jnp.take(paired, column_order, axis=2).astype(jnp.bfloat16)


def setup_inputs(seed: int = 0) -> dict:
    seeds = jax.random.split(jax.random.key(seed), 5)
    tile_list = draw_tile_list(jax.random.fold_in(seeds[4], 71), 0)
    tile_values = draw_tile_values(jax.random.fold_in(seeds[4], 71), 0)
    block_order = draw_block_order(jax.random.fold_in(seeds[4], 71), 0)
    basis = draw_basis(jax.random.fold_in(seeds[4], 71), 0)
    return {"tile_list": tile_list, "tile_values": tile_values, "block_order": block_order, "basis": basis}


def reference(tile_list, tile_values, block_order, basis):
    slot_of = jnp.zeros((NB,), jnp.int32).at[block_order].set(jnp.arange(NB, dtype=jnp.int32))
    present = tile_list[:, 0] >= 0
    first_slot = slot_of[jnp.where(present, tile_list[:, 0], 0)].astype(jnp.int32)
    second_slot = slot_of[jnp.where(present, tile_list[:, 1], 0)].astype(jnp.int32)

    def add_tile(total, item):
        tile, first, second, live = item
        weight = jnp.where(live, 1.0, 0.0).astype(jnp.float32)
        near = jnp.dot(tile.astype(jnp.float32), basis[second].astype(jnp.float32), preferred_element_type=jnp.float32) * weight
        far = jnp.dot(tile.T.astype(jnp.float32), basis[first].astype(jnp.float32), preferred_element_type=jnp.float32) * weight
        total = total.at[first].add(near)
        total = total.at[second].add(far)
        return (total, None)
    start = jnp.zeros((NB, B, K), jnp.float32)
    product, _ = lax.scan(add_tile, start, (tile_values, first_slot, second_slot, present))
    flat = product.reshape(N, K)
    scale = jnp.sqrt(jnp.float32(N))
    old = basis.reshape(N, K).astype(jnp.float32)
    projected = jnp.dot(old.T, flat, precision=lax.Precision.HIGHEST) / scale
    gram = jnp.dot(flat.T, flat, precision=lax.Precision.HIGHEST)
    first_factor = jnp.linalg.cholesky(gram)
    first_basis = lax.linalg.triangular_solve(first_factor, flat, left_side=False, lower=True, transpose_a=True)
    second = jnp.dot(first_basis.T, first_basis, precision=lax.Precision.HIGHEST)
    second_factor = jnp.linalg.cholesky(second)
    final = lax.linalg.triangular_solve(second_factor, first_basis, left_side=False, lower=True, transpose_a=True)
    basis_out = (final * scale).astype(jnp.bfloat16).reshape(NB, B, K)
    return (basis_out, projected)
```

```python
import functools

import jax
import jax.numpy as jnp
from jax import lax
from jax.experimental import pallas as pl
from jax.experimental.pallas import tpu as pltpu
from jax.sharding import PartitionSpec as P

HI = lax.Precision.HIGHEST
F32 = jnp.float32
BF16 = jnp.bfloat16
XS, CORES, YS, ZS = 4, 2, 4, 4
TILES = 16
ROWS_G, COLS_G = 32, 16
HALF = 256
RANK = 256
EDGE = 512
PACK = 384
CHUNK = PACK // (CORES * XS)


def ring(dim, step):
    if dim == "x":
        return "row", [(i, ((i // 2 + step) % 4) * 2 + i % 2) for i in range(8)]
    if dim == "core":
        return "row", [(i, i ^ 1) for i in range(8)]
    if dim == "y":
        return "col", [(i, (i // 4) * 4 + (i + step) % 4) for i in range(16)]
    return "col", [(i, ((i // 4 + step) % 4) * 4 + i % 4) for i in range(16)]


def shift(value, dim, step=0):
    axis, pairs = ring(dim, step)
    return lax.ppermute(value, axis, pairs)


def gather4(value, dim):
    half = value.shape[0] // 2
    below = shift(value, dim, 1)
    above = shift(value, dim, -1)
    far_first = shift(below[:half], dim, 1)
    far_last = shift(above[half:], dim, -1)
    return [value, below, above, far_first, far_last]


def reduce4(own, up, far, down, dim):
    half = own.shape[0] // 2
    relay_up = shift(far[:half], dim, 1)
    relay_down = shift(far[half:], dim, -1)
    early_up = shift(up[half:], dim, 1)
    early_down = shift(down[:half], dim, -1)
    late_up = shift(up[:half] + relay_up, dim, 1)
    late_down = shift(down[half:] + relay_down, dim, -1)
    return (own[:half] + late_up + early_down, own[half:] + early_up + late_down)


def exchange4(value, dim):
    got = [shift(value, dim, s) for s in (1, 2, 3)]
    return (value + got[1]) + (got[0] + got[2])


def reduce_all(keep, send):
    mine = keep + shift(send, "core")
    got = [shift(mine[s], "x", s) for s in (1, 2, 3)]
    value = (mine[0] + got[1]) + (got[0] + got[2])
    value = exchange4(value, "y")
    value = exchange4(value, "z")
    whole = jnp.stack([value] + [shift(value, "x", s) for s in (1, 2, 3)])
    return whole, shift(whole, "core")


def near_kernel(half, idx, row, col, has, tiles, side, out, tbuf, bbuf, acc, zero, tsem, bsem, osem):
    zero[...] = jnp.zeros_like(zero)

    def blank(r, c):
        @pl.when(has[r] == 0)
        def _():
            pltpu.make_async_copy(zero, out.at[r], osem.at[r]).start()

        return c

    def tile_copy(t, i):
        return pltpu.make_async_copy(tiles.at[i, pl.ds(half * HALF, HALF), :], tbuf.at[t], tsem.at[t])

    def side_copy(t, b):
        return pltpu.make_async_copy(side.at[b], bbuf.at[t], bsem.at[t])

    def load(t, c):
        @pl.when(row[t] < ROWS_G)
        def _():
            tile_copy(t, idx[t]).start()
            side_copy(t, col[t]).start()

        return c

    lax.fori_loop(0, TILES, load, 0)
    lax.fori_loop(0, ROWS_G, blank, 0)

    def work(t, slot):
        here = row[t]
        before = row[jnp.maximum(t - 1, 0)]
        after = row[jnp.minimum(t + 1, TILES - 1)]
        first = jnp.logical_or(t == 0, before != here)
        last = jnp.logical_or(t == TILES - 1, after != here)
        slot = jnp.where(first, t, slot)

        @pl.when(here < ROWS_G)
        def _():
            tile_copy(t, 0).wait()
            side_copy(t, 0).wait()
            part = jnp.dot(tbuf[t], bbuf[t], preferred_element_type=F32)

            @pl.when(first)
            def _():
                acc[slot] = part

            @pl.when(jnp.logical_not(first))
            def _():
                acc[slot] += part

            @pl.when(last)
            def _():
                pltpu.make_async_copy(acc.at[slot], out.at[here], osem.at[here]).start()

        return slot

    lax.fori_loop(0, TILES, work, jnp.int32(0))

    def finish(r, c):
        pltpu.make_async_copy(zero, out.at[r], osem.at[r]).wait()
        return c

    lax.fori_loop(0, ROWS_G, finish, 0)


def near_call(half, idx, row, col, has, tiles, side):
    smem = pl.BlockSpec(memory_space=pltpu.SMEM)
    anym = pl.BlockSpec(memory_space=pl.ANY)
    return pl.pallas_call(
        functools.partial(near_kernel, half),
        out_shape=jax.ShapeDtypeStruct((ROWS_G, HALF, RANK), F32),
        in_specs=[smem] * 4 + [anym] * 2,
        out_specs=anym,
        scratch_shapes=[
            pltpu.VMEM((TILES, HALF, EDGE), BF16),
            pltpu.VMEM((TILES, EDGE, RANK), BF16),
            pltpu.VMEM((TILES, HALF, RANK), F32),
            pltpu.VMEM((HALF, RANK), F32),
            pltpu.SemaphoreType.DMA((TILES,)),
            pltpu.SemaphoreType.DMA((TILES,)),
            pltpu.SemaphoreType.DMA((ROWS_G,)),
        ],
        compiler_params=pltpu.CompilerParams(vmem_limit_bytes=40 * 2**20),
        name="near",
    )(idx, row, col, has, tiles, side)


def far_kernel(half, idx, pos, src, unit, has, tiles, *refs):
    srcs = refs[:10]
    out, tbuf, bbuf, acc, zero, tsem, bsem, osem = refs[10:]
    zero[...] = jnp.zeros_like(zero)

    def blank(r, c):
        @pl.when(has[r] == 0)
        def _():
            pltpu.make_async_copy(zero, out.at[r], osem.at[r]).start()

        return c

    def tile_copy(t, i):
        return pltpu.make_async_copy(tiles.at[i, :, pl.ds(half * HALF, HALF)], tbuf.at[t], tsem.at[t])

    def side_copy(t, ref, u):
        return pltpu.make_async_copy(ref.at[pl.ds(u, 2)], bbuf.at[t], bsem.at[t])

    def load(t, c):
        @pl.when(pos[t] < COLS_G)
        def _():
            tile_copy(t, idx[t]).start()
            for k, ref in enumerate(srcs):
                @pl.when(src[t] == k)
                def _():
                    side_copy(t, ref, unit[t]).start()

        return c

    lax.fori_loop(0, TILES, load, 0)
    lax.fori_loop(0, COLS_G, blank, 0)

    def work(t, slot):
        here = pos[t]
        before = pos[jnp.maximum(t - 1, 0)]
        after = pos[jnp.minimum(t + 1, TILES - 1)]
        first = jnp.logical_or(t == 0, before != here)
        last = jnp.logical_or(t == TILES - 1, after != here)
        slot = jnp.where(first, t, slot)

        @pl.when(here < COLS_G)
        def _():
            tile_copy(t, 0).wait()
            side_copy(t, srcs[0], 0).wait()
            block = bbuf[t].reshape(EDGE, RANK)
            part = lax.dot_general(
                tbuf[t], block, (((0,), (0,)), ((), ())), preferred_element_type=F32
            )

            @pl.when(first)
            def _():
                acc[slot] = part

            @pl.when(jnp.logical_not(first))
            def _():
                acc[slot] += part

            @pl.when(last)
            def _():
                pltpu.make_async_copy(acc.at[slot], out.at[here], osem.at[here]).start()

        return slot

    lax.fori_loop(0, TILES, work, jnp.int32(0))

    def finish(r, c):
        pltpu.make_async_copy(zero, out.at[r], osem.at[r]).wait()
        return c

    lax.fori_loop(0, COLS_G, finish, 0)


def far_call(half, idx, pos, src, unit, has, tiles, srcs):
    smem = pl.BlockSpec(memory_space=pltpu.SMEM)
    anym = pl.BlockSpec(memory_space=pl.ANY)
    return pl.pallas_call(
        functools.partial(far_kernel, half),
        out_shape=jax.ShapeDtypeStruct((COLS_G, HALF, RANK), F32),
        in_specs=[smem] * 5 + [anym] * 11,
        out_specs=anym,
        scratch_shapes=[
            pltpu.VMEM((TILES, EDGE, HALF), BF16),
            pltpu.VMEM((TILES, 2, HALF, RANK), BF16),
            pltpu.VMEM((TILES, HALF, RANK), F32),
            pltpu.VMEM((HALF, RANK), F32),
            pltpu.SemaphoreType.DMA((TILES,)),
            pltpu.SemaphoreType.DMA((TILES,)),
            pltpu.SemaphoreType.DMA((COLS_G,)),
        ],
        compiler_params=pltpu.CompilerParams(vmem_limit_bytes=40 * 2**20),
        name="far",
    )(idx, pos, src, unit, has, tiles, *srcs)


def tdot(a, b):
    return lax.dot_general(a, b, (((0,), (0,)), ((), ())), preferred_element_type=F32, precision=HI)


def ntdot(a, b):
    return lax.dot_general(a, b, (((1,), (1,)), ((), ())), preferred_element_type=F32, precision=HI)


def hdot(a, b):
    return jnp.dot(a, b, preferred_element_type=F32, precision=HI)


def put_packed(pack, base, full):
    pack[base : base + 128, :] = full[:128, :128]
    pack[base + 128 : base + 256, :] = full[128:, :128]
    pack[base + 256 : base + 384, :] = full[128:, 128:]


def split_packed(pack, base, keep, send, at):
    place = lax.axis_index("row")
    x, core = place // CORES, place % CORES
    for s in range(XS):
        chunk = lax.rem(x + s, XS) * CHUNK
        for ref, c in ((keep, core), (send, 1 - core)):
            start = pl.multiple_of(base + c * (PACK // 2) + chunk, 8)
            ref[s, at : at + CHUNK, :] = pack[pl.ds(start, CHUNK), :]


def join_packed(pack, base, mine, other, at):
    place = lax.axis_index("row")
    x, core = place // CORES, place % CORES
    for s in range(XS):
        chunk = lax.rem(x + XS - s, XS) * CHUNK
        for ref, c in ((mine, core), (other, 1 - core)):
            start = pl.multiple_of(base + c * (PACK // 2) + chunk, 8)
            pack[pl.ds(start, CHUNK), :] = ref[s, at : at + CHUNK, :]


def take_packed(pack, base, full):
    a = pack[base : base + 128, :]
    b = pack[base + 128 : base + 256, :]
    c = pack[base + 256 : base + 384, :]
    low = lax.broadcasted_iota(jnp.int32, (128, 128), 0) >= lax.broadcasted_iota(jnp.int32, (128, 128), 1)
    full[:128, :128] = jnp.where(low, a, a.T)
    full[128:, :128] = b
    full[:128, 128:] = b.T
    full[128:, 128:] = jnp.where(low, c, c.T)


def factor64(parts, off):
    rows_in = lax.broadcasted_iota(jnp.int32, (8, 128), 0)
    parts = list(parts)
    for g in range(8):
        cols = {
            r: [jnp.broadcast_to(parts[r][:, off + 8 * g + q : off + 8 * g + q + 1], (8, 128)) for q in range(8)]
            for r in range(g, 8)
        }
        pivots = jnp.zeros((8, 128), F32)
        for q in range(8):
            pivot = jnp.broadcast_to(cols[g][q][q : q + 1, :], (8, 128))
            pivots = jnp.where(rows_in == q, pivot, pivots)
            guess = pl.reciprocal(pivot, approx=True)
            guess = guess * (2.0 - pivot * guess)
            inverse = guess * (2.0 - pivot * guess)
            line = jnp.broadcast_to(parts[g][q : q + 1, :], (8, 128)) * inverse
            heads = {w: jnp.broadcast_to(cols[g][w][q : q + 1, :], (8, 128)) for w in range(q + 1, 8)}
            for r in range(g, 8):
                factor = cols[r][q]
                if r == g:
                    factor = jnp.where(rows_in > q, factor, 0.0)
                for w in range(q + 1, 8):
                    cols[r][w] = cols[r][w] - (factor * heads[w]) * inverse
                parts[r] = parts[r] - factor * line
        parts[g] = parts[g] * lax.rsqrt(pivots)
    return parts


def factor_inverse(a_ref, w_ref):
    lanes = lax.broadcasted_iota(jnp.int32, (RANK, RANK), 1)
    rows = lax.broadcasted_iota(jnp.int32, (RANK, RANK), 0)
    w_ref[...] = jnp.where(rows == lanes, 1.0, 0.0).astype(F32)
    lane = lax.broadcasted_iota(jnp.int32, (8, 128), 1)
    row8 = lax.broadcasted_iota(jnp.int32, (8, 128), 0)
    for k in range(4):
        lo, group = 64 * k, 128 * (k // 2)
        off = 64 * (k % 2)
        eye_off = 64 - off
        in_block = jnp.logical_and(lane >= off, lane < off + 64)
        parts = []
        for r in range(8):
            piece = a_ref[lo + 8 * r : lo + 8 * r + 8, group : group + 128]
            eye = jnp.where(lane - eye_off == row8 + 8 * r, 1.0, 0.0).astype(F32)
            parts.append(jnp.where(in_block, piece, eye))
        parts = factor64(parts, off)
        kept = [jnp.where(in_block, 0.0, part) for part in parts]
        block = jnp.concatenate(kept, axis=0)
        turned = pltpu.roll(block, 64, 1)
        at_block, at_zero = (turned, turned) if off == 0 else (turned, block)
        w_here = hdot(at_zero[:, :64], w_ref[lo : lo + 64, :])
        w_ref[lo : lo + 64, :] = w_here
        if k < 3:
            start = 128 * ((k + 1) // 2)
            panel = ntdot(a_ref[start:, group : group + 128], at_block)
            a_ref[start:, start:] = a_ref[start:, start:] - ntdot(panel, panel)
            rest = lo + 64
            w_ref[rest:, :] = w_ref[rest:, :] - hdot(panel[rest - start :, :], w_here)


def gram_kernel(row0, col0, row1, col1, old, prod, keep, send, pack):
    for h, (r, c) in enumerate(((row0, col0), (row1, col1))):
        for b in range(2):
            prod[b * EDGE + h * HALF : b * EDGE + (h + 1) * HALF, :] = r[b] + c[b]
    value = prod[...]
    put_packed(pack, 0, tdot(value, value))
    split_packed(pack, 0, keep, send, 0)
    scale = jnp.sqrt(F32(131072.0))
    put_packed(pack, 0, tdot(old[...].reshape(2 * EDGE, RANK).astype(F32), value) / scale)
    split_packed(pack, 0, keep, send, CHUNK)


def first_kernel(mine, other, prod, first, keep, send, pack, a_ref, w_ref):
    join_packed(pack, 0, mine, other, 0)
    take_packed(pack, 0, a_ref)
    factor_inverse(a_ref, w_ref)
    value = ntdot(prod[...], w_ref[...])
    first[...] = value
    put_packed(pack, 0, tdot(value, value))
    split_packed(pack, 0, keep, send, 0)


def last_kernel(mine, other, gmine, gother, first, out, proj, pack, a_ref, w_ref):
    join_packed(pack, 0, gmine, gother, CHUNK)
    take_packed(pack, 0, proj)
    join_packed(pack, 0, mine, other, 0)
    take_packed(pack, 0, a_ref)
    factor_inverse(a_ref, w_ref)
    scale = jnp.sqrt(F32(131072.0))
    value = ntdot(first[...], w_ref[...]) * scale
    out[...] = value.astype(BF16).reshape(2, EDGE, RANK)


def dense_call(kernel, outs, scratch, name, *args):
    vm = pl.BlockSpec(memory_space=pltpu.VMEM)
    return pl.pallas_call(
        kernel,
        out_shape=[jax.ShapeDtypeStruct(s, d) for s, d in outs],
        in_specs=[vm] * len(args),
        out_specs=[vm] * len(outs),
        scratch_shapes=[pltpu.VMEM(s, F32) for s in scratch],
        compiler_params=pltpu.CompilerParams(vmem_limit_bytes=32 * 2**20),
        name=name,
    )(*args)


def ranked(key, *values):
    n = key.shape[0]
    where = jnp.arange(n, dtype=jnp.int32)
    before = (key[None, :] < key[:, None]) | ((key[None, :] == key[:, None]) & (where[None, :] < where[:, None]))
    rank = jnp.sum(before.astype(jnp.int32), axis=1)
    pick = rank[None, :] == where[:, None]
    return [jnp.sum(jnp.where(pick, v[None, :], 0), axis=1) for v in (key, where) + values]


def per_device(tile_list, tile_values, block_order, basis):
    row_here = lax.axis_index("row")
    col_here = lax.axis_index("col")
    x_here, core_here = row_here // 2, row_here % 2
    z_here, y_here = col_here // 4, col_here % 4

    side = lax.all_gather(basis, "row", axis=0, tiled=True)

    slot_range = jnp.arange(256, dtype=jnp.int32)
    present = tile_list[:, 0] >= 0
    match = block_order[None, None, :] == tile_list[:, :, None]
    slots = jnp.sum(jnp.where(match, slot_range[None, None, :], 0), axis=2)
    first_slot, second_slot = slots[:, 0], slots[:, 1]
    row_local = jnp.where(present, first_slot - row_here * ROWS_G, ROWS_G)
    second_owner = second_slot // 2
    second_row = second_owner // 16
    col_local = jnp.where(present, second_row * 2 + second_slot % 2, 0)
    second_x, second_core = second_row // 2, second_row % 2
    col_pos = (second_core ^ core_here) * 8 + ((second_x - x_here) % 4) * 2 + second_slot % 2
    col_pos = jnp.where(present, col_pos, COLS_G)
    n_row, n_idx, n_col = ranked(row_local, col_local)
    n_has = jnp.sum((row_local[None, :] == jnp.arange(ROWS_G)[:, None]).astype(jnp.int32), axis=1)
    f_has = jnp.sum((col_pos[None, :] == jnp.arange(COLS_G)[:, None]).astype(jnp.int32), axis=1)
    first_owner = (first_slot // 2) % 16
    dz = (first_owner // 4 - z_here) % 4
    dy = (first_owner % 4 - y_here) % 4
    odd = first_slot % 2
    outer = jnp.where(odd == 0, dz, dy)
    inner = jnp.where(odd == 0, dy, dz)
    spot = jnp.where(inner == 0, 0, jnp.where(inner == 3, 2, jnp.where(inner == 1, 4, 6)))
    kind = jnp.where(outer == 0, 0, jnp.where(outer == 3, 1, jnp.where(outer == 1, 2, jnp.where(spot < 4, 3, 4))))
    unit = jnp.where(kind == 4, spot - 4, spot)
    f_pos, f_idx, f_src, f_unit = ranked(col_pos, kind + 5 * odd, unit)

    even_own = basis[0].reshape(2, HALF, RANK)
    odd_own = basis[1].reshape(2, HALF, RANK)
    even = gather4(even_own, "y")
    odd_part = gather4(odd_own, "z")
    even = gather4(jnp.concatenate(even, axis=0), "z")
    odd_part = gather4(jnp.concatenate(odd_part, axis=0), "y")

    near = [near_call(h, n_idx, n_row, n_col, n_has, tile_values, side) for h in range(2)]
    row_owned = [lax.psum_scatter(n, "col", scatter_dimension=0, tiled=True) for n in near]
    col_owned = []
    for h in range(2):
        far = far_call(h, f_idx, f_pos, f_src, f_unit, f_has, tile_values, even + odd_part)
        far = far.reshape(2, 4, 2, HALF, RANK)
        chip = far[0] + shift(far[1], "core")
        col_owned.append(jnp.concatenate(reduce4(chip[0], chip[1], chip[2], chip[3], "x"), axis=0))

    product, keep, send = dense_call(
        gram_kernel,
        [((2 * EDGE, RANK), F32), ((4, 2 * CHUNK, 128), F32), ((4, 2 * CHUNK, 128), F32)],
        [(PACK, 128)],
        "gram",
        row_owned[0],
        col_owned[0],
        row_owned[1],
        col_owned[1],
        basis,
    )
    gmine, gother = reduce_all(keep, send)
    first, keep, send = dense_call(
        first_kernel,
        [((2 * EDGE, RANK), F32), ((4, CHUNK, 128), F32), ((4, CHUNK, 128), F32)],
        [(PACK, 128), (RANK, RANK), (RANK, RANK)],
        "first",
        gmine,
        gother,
        product,
    )
    mine, other = reduce_all(keep, send)
    basis_out, projected = dense_call(
        last_kernel,
        [((2, EDGE, RANK), BF16), ((RANK, RANK), F32)],
        [(PACK, 128), (RANK, RANK), (RANK, RANK)],
        "last",
        mine,
        other,
        gmine,
        gother,
        first,
    )
    return (basis_out, projected)


def solution(mesh):
    in_specs = (
        P(("row", "col"), None),
        P(("row", "col"), None, None),
        P(),
        P(("row", "col"), None, None),
    )
    out_specs = (P(("row", "col"), None, None), P())
    return jax.shard_map(per_device, mesh=mesh, in_specs=in_specs, out_specs=out_specs, check_vma=False)
```

```python
import jax
import jax.numpy as jnp
from jax import lax
from jax.experimental import pallas as pl
from jax.experimental.pallas import tpu as pltpu
from jax.sharding import PartitionSpec as P

HI = lax.Precision.HIGHEST
F32 = jnp.float32
BF16 = jnp.bfloat16
XS, CORES, YS, ZS = 4, 2, 4, 4
TILES = 16
ROWS_G, COLS_G = 32, 16
HALF = 256
RANK = 256
EDGE = 512
PACK = 384
CHUNK = PACK // (CORES * XS)
BOUND = 2.0**20


def ring(dim, step):
    if dim == "x":
        return "row", [(i, ((i // 2 + step) % 4) * 2 + i % 2) for i in range(8)]
    if dim == "core":
        return "row", [(i, i ^ 1) for i in range(8)]
    if dim == "y":
        return "col", [(i, (i // 4) * 4 + (i + step) % 4) for i in range(16)]
    return "col", [(i, ((i // 4 + step) % 4) * 4 + i % 4) for i in range(16)]


def shift(value, dim, step=0):
    axis, pairs = ring(dim, step)
    return lax.ppermute(value, axis, pairs)


def gather4(value, dim):
    half = value.shape[0] // 2
    below = shift(value, dim, 1)
    above = shift(value, dim, -1)
    far_first = shift(below[:half], dim, 1)
    far_last = shift(above[half:], dim, -1)
    return [value, below, above, far_first, far_last]


def reduce4(own, up, far, down, dim):
    half = own.shape[0] // 2
    relay_up = shift(far[:half], dim, 1)
    relay_down = shift(far[half:], dim, -1)
    early_up = shift(up[half:], dim, 1)
    early_down = shift(down[:half], dim, -1)
    late_up = shift(up[:half] + relay_up, dim, 1)
    late_down = shift(down[half:] + relay_down, dim, -1)
    return (own[:half] + late_up + early_down, own[half:] + early_up + late_down)


def exchange4(value, dim):
    got = [shift(value, dim, s) for s in (1, 2, 3)]
    return (value + got[1]) + (got[0] + got[2])


def reduce_all(keep, send):
    mine = keep + shift(send, "core")
    got = [shift(mine[s], "x", s) for s in (1, 2, 3)]
    value = (mine[0] + got[1]) + (got[0] + got[2])
    value = exchange4(value, "y")
    value = exchange4(value, "z")
    whole = jnp.stack([value] + [shift(value, "x", s) for s in (1, 2, 3)])
    return whole, shift(whole, "core")


def in_hbm(value):
    return pltpu.with_memory_space_constraint(value, pltpu.HBM)


def near_kernel(idx, row, col, has, tiles, side, out, token, tbuf, bbuf, acc, zero, tsem, bsem, osem):
    zero[...] = jnp.zeros_like(zero)

    def blank(r, c):
        @pl.when(has[r] == 0)
        def _():
            pltpu.make_async_copy(zero, out.at[r], osem.at[r]).start()

        return c

    def tile_copy(t, i):
        return pltpu.make_async_copy(tiles.at[i], tbuf.at[t], tsem.at[t])

    def side_copy(t, b):
        return pltpu.make_async_copy(side.at[b], bbuf.at[t], bsem.at[t])

    def load(t, c):
        @pl.when(row[t] < ROWS_G)
        def _():
            tile_copy(t, idx[t]).start()
            side_copy(t, col[t]).start()

        return c

    lax.fori_loop(0, TILES, load, 0)
    lax.fori_loop(0, ROWS_G, blank, 0)

    def work(t, slot):
        here = row[t]
        before = row[jnp.maximum(t - 1, 0)]
        after = row[jnp.minimum(t + 1, TILES - 1)]
        first = jnp.logical_or(t == 0, before != here)
        last = jnp.logical_or(t == TILES - 1, after != here)
        slot = jnp.where(first, t, slot)

        @pl.when(here < ROWS_G)
        def _():
            tile_copy(t, 0).wait()
            side_copy(t, 0).wait()
            part = jnp.dot(tbuf[t], bbuf[t], preferred_element_type=F32)

            @pl.when(first)
            def _():
                acc[slot] = part

            @pl.when(jnp.logical_not(first))
            def _():
                acc[slot] += part

            @pl.when(last)
            def _():
                pltpu.make_async_copy(acc.at[slot], out.at[here], osem.at[here]).start()

        return slot

    lax.fori_loop(0, TILES, work, jnp.int32(0))

    def finish(r, c):
        pltpu.make_async_copy(zero, out.at[r], osem.at[r]).wait()
        return c

    lax.fori_loop(0, ROWS_G, finish, 0)
    token[...] = jnp.zeros_like(token)


def near_call(idx, row, col, has, tiles, side):
    smem = pl.BlockSpec(memory_space=pltpu.SMEM)
    hbm = pl.BlockSpec(memory_space=pltpu.HBM)
    return pl.pallas_call(
        near_kernel,
        out_shape=[jax.ShapeDtypeStruct((ROWS_G, EDGE, RANK), F32), jax.ShapeDtypeStruct((8, 128), F32)],
        in_specs=[smem] * 4 + [hbm] * 2,
        out_specs=[hbm, pl.BlockSpec(memory_space=pltpu.VMEM)],
        scratch_shapes=[
            pltpu.VMEM((TILES, EDGE, EDGE), BF16),
            pltpu.VMEM((TILES, EDGE, RANK), BF16),
            pltpu.VMEM((TILES, EDGE, RANK), F32),
            pltpu.VMEM((EDGE, RANK), F32),
            pltpu.SemaphoreType.DMA((TILES,)),
            pltpu.SemaphoreType.DMA((TILES,)),
            pltpu.SemaphoreType.DMA((ROWS_G,)),
        ],
        compiler_params=pltpu.CompilerParams(vmem_limit_bytes=40 * 2**20),
        name="near",
    )(idx, row, col, has, in_hbm(tiles), in_hbm(side))


def far_kernel(idx, pos, src, unit, has, tiles, *refs):
    srcs = refs[:10]
    out, tbuf, bbuf, acc, zero, tsem, bsem, osem = refs[10:]
    zero[...] = jnp.zeros_like(zero)

    def blank(r, c):
        @pl.when(has[r] == 0)
        def _():
            pltpu.make_async_copy(zero, out.at[r], osem.at[r]).start()

        return c

    def tile_copy(t, i):
        return pltpu.make_async_copy(tiles.at[i], tbuf.at[t], tsem.at[t])

    def side_copy(t, ref, u):
        return pltpu.make_async_copy(ref.at[pl.ds(u, 2)], bbuf.at[t], bsem.at[t])

    def load(t, c):
        @pl.when(pos[t] < COLS_G)
        def _():
            tile_copy(t, idx[t]).start()
            for k, ref in enumerate(srcs):
                @pl.when(src[t] == k)
                def _():
                    side_copy(t, ref, unit[t]).start()

        return c

    lax.fori_loop(0, TILES, load, 0)
    lax.fori_loop(0, COLS_G, blank, 0)

    def work(t, slot):
        here = pos[t]
        before = pos[jnp.maximum(t - 1, 0)]
        after = pos[jnp.minimum(t + 1, TILES - 1)]
        first = jnp.logical_or(t == 0, before != here)
        last = jnp.logical_or(t == TILES - 1, after != here)
        slot = jnp.where(first, t, slot)

        @pl.when(here < COLS_G)
        def _():
            tile_copy(t, 0).wait()
            side_copy(t, srcs[0], 0).wait()
            block = bbuf[t].reshape(EDGE, RANK)
            part = lax.dot_general(
                tbuf[t], block, (((0,), (0,)), ((), ())), preferred_element_type=F32
            )

            @pl.when(first)
            def _():
                acc[slot] = part

            @pl.when(jnp.logical_not(first))
            def _():
                acc[slot] += part

            @pl.when(last)
            def _():
                pltpu.make_async_copy(acc.at[slot], out.at[here], osem.at[here]).start()

        return slot

    lax.fori_loop(0, TILES, work, jnp.int32(0))

    def finish(r, c):
        pltpu.make_async_copy(zero, out.at[r], osem.at[r]).wait()
        return c

    lax.fori_loop(0, COLS_G, finish, 0)


def far_call(idx, pos, src, unit, has, tiles, srcs):
    smem = pl.BlockSpec(memory_space=pltpu.SMEM)
    anym = pl.BlockSpec(memory_space=pl.ANY)
    return pl.pallas_call(
        far_kernel,
        out_shape=jax.ShapeDtypeStruct((COLS_G, EDGE, RANK), F32),
        in_specs=[smem] * 5 + [anym] * 11,
        out_specs=anym,
        scratch_shapes=[
            pltpu.VMEM((TILES, EDGE, EDGE), BF16),
            pltpu.VMEM((TILES, 2, HALF, RANK), BF16),
            pltpu.VMEM((TILES, EDGE, RANK), F32),
            pltpu.VMEM((EDGE, RANK), F32),
            pltpu.SemaphoreType.DMA((TILES,)),
            pltpu.SemaphoreType.DMA((TILES,)),
            pltpu.SemaphoreType.DMA((COLS_G,)),
        ],
        compiler_params=pltpu.CompilerParams(vmem_limit_bytes=40 * 2**20),
        name="far",
    )(idx, pos, src, unit, has, in_hbm(tiles), *srcs)


def tdot(a, b):
    return lax.dot_general(a, b, (((0,), (0,)), ((), ())), preferred_element_type=F32, precision=HI)


def ntdot(a, b):
    return lax.dot_general(a, b, (((1,), (1,)), ((), ())), preferred_element_type=F32, precision=HI)


def hdot(a, b):
    return jnp.dot(a, b, preferred_element_type=F32, precision=HI)


def put_packed(pack, base, full):
    pack[base : base + 128, :] = full[:128, :128]
    pack[base + 128 : base + 256, :] = full[128:, :128]
    pack[base + 256 : base + 384, :] = full[128:, 128:]


def split_packed(pack, base, keep, send, at):
    place = lax.axis_index("row")
    x, core = place // CORES, place % CORES
    for s in range(XS):
        chunk = lax.rem(x + s, XS) * CHUNK
        for ref, c in ((keep, core), (send, 1 - core)):
            start = pl.multiple_of(base + c * (PACK // 2) + chunk, 8)
            ref[s, at : at + CHUNK, :] = pack[pl.ds(start, CHUNK), :]


def join_packed(pack, base, mine, other, at):
    place = lax.axis_index("row")
    x, core = place // CORES, place % CORES
    for s in range(XS):
        chunk = lax.rem(x + XS - s, XS) * CHUNK
        for ref, c in ((mine, core), (other, 1 - core)):
            start = pl.multiple_of(base + c * (PACK // 2) + chunk, 8)
            pack[pl.ds(start, CHUNK), :] = ref[s, at : at + CHUNK, :]


def take_packed(pack, base, full):
    a = pack[base : base + 128, :]
    b = pack[base + 128 : base + 256, :]
    c = pack[base + 256 : base + 384, :]
    low = lax.broadcasted_iota(jnp.int32, (128, 128), 0) >= lax.broadcasted_iota(jnp.int32, (128, 128), 1)
    full[:128, :128] = jnp.where(low, a, a.T)
    full[128:, :128] = b
    full[:128, 128:] = b.T
    full[128:, 128:] = jnp.where(low, c, c.T)


def factor64(parts, off):
    rows_in = lax.broadcasted_iota(jnp.int32, (8, 128), 0)
    parts = list(parts)
    for g in range(8):
        cols = {
            r: [jnp.broadcast_to(parts[r][:, off + 8 * g + q : off + 8 * g + q + 1], (8, 128)) for q in range(8)]
            for r in range(g, 8)
        }
        pivots = jnp.zeros((8, 128), F32)
        for q in range(8):
            pivot = jnp.broadcast_to(cols[g][q][q : q + 1, :], (8, 128))
            pivots = jnp.where(rows_in == q, pivot, pivots)
            guess = pl.reciprocal(pivot, approx=True)
            guess = guess * (2.0 - pivot * guess)
            inverse = guess * (2.0 - pivot * guess)
            line = jnp.broadcast_to(parts[g][q : q + 1, :], (8, 128)) * inverse
            heads = {w: jnp.broadcast_to(cols[g][w][q : q + 1, :], (8, 128)) for w in range(q + 1, 8)}
            for r in range(g, 8):
                factor = cols[r][q]
                if r == g:
                    factor = jnp.where(rows_in > q, factor, 0.0)
                for w in range(q + 1, 8):
                    cols[r][w] = cols[r][w] - (factor * heads[w]) * inverse
                parts[r] = parts[r] - factor * line
        parts[g] = parts[g] * lax.rsqrt(pivots)
    return parts


def factor_inverse(a_ref, w_ref):
    lanes = lax.broadcasted_iota(jnp.int32, (RANK, RANK), 1)
    rows = lax.broadcasted_iota(jnp.int32, (RANK, RANK), 0)
    w_ref[...] = jnp.where(rows == lanes, 1.0, 0.0).astype(F32)
    lane = lax.broadcasted_iota(jnp.int32, (8, 128), 1)
    row8 = lax.broadcasted_iota(jnp.int32, (8, 128), 0)
    for k in range(4):
        lo, group = 64 * k, 128 * (k // 2)
        off = 64 * (k % 2)
        eye_off = 64 - off
        in_block = jnp.logical_and(lane >= off, lane < off + 64)
        parts = []
        for r in range(8):
            piece = a_ref[lo + 8 * r : lo + 8 * r + 8, group : group + 128]
            eye = jnp.where(lane - eye_off == row8 + 8 * r, 1.0, 0.0).astype(F32)
            parts.append(jnp.where(in_block, piece, eye))
        parts = factor64(parts, off)
        kept = [jnp.where(in_block, 0.0, part) for part in parts]
        block = jnp.concatenate(kept, axis=0)
        turned = pltpu.roll(block, 64, 1)
        at_block, at_zero = (turned, turned) if off == 0 else (turned, block)
        w_here = hdot(at_zero[:, :64], w_ref[lo : lo + 64, :])
        w_ref[lo : lo + 64, :] = w_here
        if k < 3:
            start = 128 * ((k + 1) // 2)
            panel = ntdot(a_ref[start:, group : group + 128], at_block)
            a_ref[start:, start:] = a_ref[start:, start:] - ntdot(panel, panel)
            rest = lo + 64
            w_ref[rest:, :] = w_ref[rest:, :] - hdot(panel[rest - start :, :], w_here)


def old_gram_kernel(side, token, half, pack):
    del token
    gram = jnp.zeros((RANK, RANK), F32)
    for b in range(COLS_G):
        value = side[b]
        gram += lax.dot_general(value, value, (((0,), (0,)), ((), ())), preferred_element_type=F32)
    put_packed(pack, 0, gram)
    core = lax.rem(lax.axis_index("row"), CORES)
    half[...] = pack[pl.ds(pl.multiple_of(core * (PACK // 2), 8), PACK // 2), :]


def old_factor_kernel(mine, other, w_out, pack, a_ref, w_ref):
    core = lax.rem(lax.axis_index("row"), CORES)
    for ref, c in ((mine, core), (other, 1 - core)):
        pack[pl.ds(pl.multiple_of(c * (PACK // 2), 8), PACK // 2), :] = ref[...]
    take_packed(pack, 0, a_ref)
    factor_inverse(a_ref, w_ref)
    w_out[...] = w_ref[...] * jnp.sqrt(F32(131072.0))


def apply_kernel(row, col, old, w, prod, first, keep, send, pack):
    value = row[...].reshape(2 * EDGE, RANK) + col[...].reshape(2 * EDGE, RANK)
    prod[...] = value
    scale = jnp.sqrt(F32(131072.0))
    put_packed(pack, 0, tdot(old[...].reshape(2 * EDGE, RANK).astype(F32), value) / scale)
    split_packed(pack, 0, keep, send, CHUNK)
    better = ntdot(value, w[...])
    first[...] = better
    put_packed(pack, 0, tdot(better, better))
    split_packed(pack, 0, keep, send, 0)


def gram_kernel(prod, keep, send, pack):
    value = prod[...]
    put_packed(pack, 0, tdot(value, value))
    split_packed(pack, 0, keep, send, 0)


def first_kernel(mine, other, prod, first, keep, send, pack, a_ref, w_ref):
    join_packed(pack, 0, mine, other, 0)
    take_packed(pack, 0, a_ref)
    factor_inverse(a_ref, w_ref)
    value = ntdot(prod[...], w_ref[...])
    first[...] = value
    put_packed(pack, 0, tdot(value, value))
    split_packed(pack, 0, keep, send, 0)


def diagonal_sum(value):
    spot = lax.broadcasted_iota(jnp.int32, value.shape, 0) == lax.broadcasted_iota(jnp.int32, value.shape, 1)
    return jnp.sum(jnp.where(spot, value, 0.0))


def last_kernel(mine, other, first, out, pack, a_ref, w_ref):
    join_packed(pack, 0, mine, other, 0)
    take_packed(pack, 0, a_ref)
    factor_inverse(a_ref, w_ref)
    scale = jnp.sqrt(F32(131072.0))
    value = ntdot(first[...], w_ref[...]) * scale
    out[...] = value.astype(BF16).reshape(2, EDGE, RANK)


def end_kernel(mine, other, first, out, proj, flag, pack, a_ref, w_ref):
    join_packed(pack, 0, mine, other, CHUNK)
    take_packed(pack, 0, proj)
    join_packed(pack, 0, mine, other, 0)
    take_packed(pack, 0, a_ref)
    size = diagonal_sum(a_ref[...])
    factor_inverse(a_ref, w_ref)
    w = w_ref[...]
    good = (size * jnp.sum(w * w) <= BOUND) & (size > 1e-25) & (size < 1e30)
    flag[0] = good.astype(jnp.int32)
    scale = jnp.sqrt(F32(131072.0))
    value = ntdot(first[...], w) * scale
    out[...] = value.astype(BF16).reshape(2, EDGE, RANK)


def dense_call(kernel, outs, scratch, name, *args):
    vm = pl.BlockSpec(memory_space=pltpu.VMEM)
    return pl.pallas_call(
        kernel,
        out_shape=[jax.ShapeDtypeStruct(s, d) for s, d in outs],
        in_specs=[vm] * len(args),
        out_specs=[pl.BlockSpec(memory_space=pltpu.SMEM) if s == (1,) else vm for s, _ in outs],
        scratch_shapes=[pltpu.VMEM(s, F32) for s in scratch],
        compiler_params=pltpu.CompilerParams(vmem_limit_bytes=32 * 2**20),
        name=name,
    )(*args)


def ranked(key, *values):
    n = key.shape[0]
    where = jnp.arange(n, dtype=jnp.int32)
    before = (key[None, :] < key[:, None]) | ((key[None, :] == key[:, None]) & (where[None, :] < where[:, None]))
    rank = jnp.sum(before.astype(jnp.int32), axis=1)
    pick = rank[None, :] == where[:, None]
    return [jnp.sum(jnp.where(pick, v[None, :], 0), axis=1) for v in (key, where) + values]


def per_device(tile_list, tile_values, block_order, basis):
    row_here = lax.axis_index("row")
    col_here = lax.axis_index("col")
    x_here, core_here = row_here // 2, row_here % 2
    z_here, y_here = col_here // 4, col_here % 4

    side = lax.all_gather(basis, "row", axis=0, tiled=True)

    slot_range = jnp.arange(256, dtype=jnp.int32)
    present = tile_list[:, 0] >= 0
    match = block_order[None, None, :] == tile_list[:, :, None]
    slots = jnp.sum(jnp.where(match, slot_range[None, None, :], 0), axis=2)
    first_slot, second_slot = slots[:, 0], slots[:, 1]
    row_local = jnp.where(present, first_slot - row_here * ROWS_G, ROWS_G)
    second_owner = second_slot // 2
    second_row = second_owner // 16
    col_local = jnp.where(present, second_row * 2 + second_slot % 2, 0)
    second_x, second_core = second_row // 2, second_row % 2
    col_pos = (second_core ^ core_here) * 8 + ((second_x - x_here) % 4) * 2 + second_slot % 2
    col_pos = jnp.where(present, col_pos, COLS_G)
    n_row, n_idx, n_col = ranked(row_local, col_local)
    n_has = jnp.sum((row_local[None, :] == jnp.arange(ROWS_G)[:, None]).astype(jnp.int32), axis=1)
    f_has = jnp.sum((col_pos[None, :] == jnp.arange(COLS_G)[:, None]).astype(jnp.int32), axis=1)
    first_owner = (first_slot // 2) % 16
    dz = (first_owner // 4 - z_here) % 4
    dy = (first_owner % 4 - y_here) % 4
    odd = first_slot % 2
    outer = jnp.where(odd == 0, dz, dy)
    inner = jnp.where(odd == 0, dy, dz)
    spot = jnp.where(inner == 0, 0, jnp.where(inner == 3, 2, jnp.where(inner == 1, 4, 6)))
    kind = jnp.where(outer == 0, 0, jnp.where(outer == 3, 1, jnp.where(outer == 1, 2, jnp.where(spot < 4, 3, 4))))
    unit = jnp.where(kind == 4, spot - 4, spot)
    f_pos, f_idx, f_src, f_unit = ranked(col_pos, kind + 5 * odd, unit)

    even_own = basis[0].reshape(2, HALF, RANK)
    odd_own = basis[1].reshape(2, HALF, RANK)
    even = gather4(even_own, "y")
    odd_part = gather4(odd_own, "z")
    even = gather4(jnp.concatenate(even, axis=0), "z")
    odd_part = gather4(jnp.concatenate(odd_part, axis=0), "y")
    side, even[:3], odd_part[:3] = lax.optimization_barrier((side, even[:3], odd_part[:3]))
    near, token = near_call(n_idx, n_row, n_col, n_has, tile_values, side)
    row_owned = lax.psum_scatter(near, "col", scatter_dimension=0, tiled=True)

    far = far_call(f_idx, f_pos, f_src, f_unit, f_has, tile_values, even + odd_part)
    far = far.reshape(2, 4, 2, EDGE, RANK)
    chip = far[0] + shift(far[1], "core")
    col_owned = jnp.concatenate(reduce4(chip[0], chip[1], chip[2], chip[3], "x"), axis=0)

    halves = [((4, CHUNK, 128), F32)] * 2
    squares = [(PACK, 128), (RANK, RANK), (RANK, RANK)]
    tall = ((2 * EDGE, RANK), F32)
    (half,) = dense_call(old_gram_kernel, [((PACK // 2, 128), F32)], [(PACK, 128)], "old_gram", side, token)
    half = exchange4(exchange4(half, "y"), "z")
    mine, other = half, shift(half, "core")
    (w,) = dense_call(old_factor_kernel, [((RANK, RANK), F32)], squares, "old_factor", mine, other)
    product, first, keep, send = dense_call(
        apply_kernel,
        [tall, tall] + [((4, 2 * CHUNK, 128), F32)] * 2,
        [(PACK, 128)],
        "apply",
        row_owned,
        col_owned,
        basis,
        w,
    )
    mine, other = reduce_all(keep, send)
    wide = ((2, EDGE, RANK), BF16)
    quick, projected, flag = dense_call(
        end_kernel, [wide, ((RANK, RANK), F32), ((1,), jnp.int32)], squares, "end", mine, other, first
    )

    def two_passes(product):
        keep, send = dense_call(gram_kernel, halves, [(PACK, 128)], "gram", product)
        mine, other = reduce_all(keep, send)
        first, keep, send = dense_call(first_kernel, [tall] + halves, squares, "first", mine, other, product)
        mine, other = reduce_all(keep, send)
        return dense_call(last_kernel, [wide], squares, "last", mine, other, first)[0]

    basis_out = lax.cond(flag[0] == 1, lambda p: quick, two_passes, product)
    return (basis_out, projected)


def solution(mesh):
    in_specs = (
        P(("row", "col"), None),
        P(("row", "col"), None, None),
        P(),
        P(("row", "col"), None, None),
    )
    out_specs = (P(("row", "col"), None, None), P())
    return jax.shard_map(per_device, mesh=mesh, in_specs=in_specs, out_specs=out_specs, check_vma=False)
```

```python
import jax
import jax.numpy as jnp
from jax import lax
from jax.experimental import pallas as pl
from jax.experimental.pallas import tpu as pltpu
from jax.sharding import PartitionSpec as P

HI = lax.Precision.HIGHEST
F32 = jnp.float32
BF16 = jnp.bfloat16
XS, CORES, YS, ZS = 4, 2, 4, 4
TILES = 16
ROWS_G, COLS_G = 32, 16
HALF = 256
RANK = 256
EDGE = 512
PACK = 384
CHUNK = PACK // (CORES * XS)
BOUND = 2.0**20
CLOSE = 1e-6


def ring(dim, step):
    if dim == "x":
        return "row", [(i, ((i // 2 + step) % 4) * 2 + i % 2) for i in range(8)]
    if dim == "core":
        return "row", [(i, i ^ 1) for i in range(8)]
    if dim == "y":
        return "col", [(i, (i // 4) * 4 + (i + step) % 4) for i in range(16)]
    return "col", [(i, ((i // 4 + step) % 4) * 4 + i % 4) for i in range(16)]


def shift(value, dim, step=0):
    axis, pairs = ring(dim, step)
    return lax.ppermute(value, axis, pairs)


def gather_plane(basis):
    own = basis.reshape(4, HALF, RANK)
    y_below, y_above = shift(own, "y", 1), shift(own, "y", -1)
    z_below, z_above = shift(own, "z", 1), shift(own, "z", -1)
    lines = []
    for odd, first, near in ((0, "y", (y_below, y_above)), (1, "z", (z_below, z_above))):
        lo = 2 * odd
        opposite = [shift(near[0][lo : lo + 1], first, 1), shift(near[1][lo + 1 : lo + 2], first, -1)]
        line = jnp.concatenate([near[0][lo : lo + 2], near[1][lo : lo + 2]] + opposite, axis=0)
        lines.append(line)
    groups = [
        (far, line, shift(line, second, 1), shift(line, second, -1))
        for far, line, second in zip(((z_below, z_above), (y_below, y_above)), lines, "zy")
    ]
    return own, groups


def finish_plane(own, groups):
    found = [own]
    for lo, second, (far, line, below, above) in zip((0, 2), "zy", groups):
        low = shift(jnp.concatenate([far[0][lo : lo + 2], below[:2]], axis=0), second, 1)
        high = shift(above[2:], second, -1)
        found += [line, far[0], below, far[1], above, low, high]
    return found


def reduce4(own, up, far, down, dim):
    half = own.shape[0] // 2
    relay_up = shift(far[:half], dim, 1)
    relay_down = shift(far[half:], dim, -1)
    early_up = shift(up[half:], dim, 1)
    early_down = shift(down[:half], dim, -1)
    late_up = shift(up[:half] + relay_up, dim, 1)
    late_down = shift(down[half:] + relay_down, dim, -1)
    return (own[:half] + late_up + early_down, own[half:] + early_up + late_down)


def exchange4(value, dim):
    got = [shift(value, dim, s) for s in (1, 2, 3)]
    return (value + got[1]) + (got[0] + got[2])


def reduce_all(keep, send):
    mine = keep + shift(send, "core")
    got = [shift(mine[s], "x", s) for s in (1, 2, 3)]
    value = (mine[0] + got[1]) + (got[0] + got[2])
    value = exchange4(value, "y")
    value = exchange4(value, "z")
    whole = jnp.stack([value] + [shift(value, "x", s) for s in (1, 2, 3)])
    return whole, shift(whole, "core")


def in_hbm(value):
    return pltpu.with_memory_space_constraint(value, pltpu.HBM)


def near_kernel(idx, row, col, has, tiles, side, out, token, tbuf, bbuf, acc, zero, tsem, bsem, osem):
    zero[...] = jnp.zeros_like(zero)

    def blank(r, c):
        @pl.when(has[r] == 0)
        def _():
            pltpu.make_async_copy(zero, out.at[r], osem.at[r]).start()

        return c

    def tile_copy(t, i):
        return pltpu.make_async_copy(tiles.at[i], tbuf.at[t], tsem.at[t])

    def side_copy(t, b):
        return pltpu.make_async_copy(side.at[b], bbuf.at[t], bsem.at[t])

    def load(t, c):
        @pl.when(row[t] < ROWS_G)
        def _():
            tile_copy(t, idx[t]).start()
            side_copy(t, col[t]).start()

        return c

    lax.fori_loop(0, TILES, load, 0)
    lax.fori_loop(0, ROWS_G, blank, 0)

    def work(t, slot):
        here = row[t]
        before = row[jnp.maximum(t - 1, 0)]
        after = row[jnp.minimum(t + 1, TILES - 1)]
        first = jnp.logical_or(t == 0, before != here)
        last = jnp.logical_or(t == TILES - 1, after != here)
        slot = jnp.where(first, t, slot)

        @pl.when(here < ROWS_G)
        def _():
            tile_copy(t, 0).wait()
            side_copy(t, 0).wait()
            part = jnp.dot(tbuf[t], bbuf[t], preferred_element_type=F32)

            @pl.when(first)
            def _():
                acc[slot] = part

            @pl.when(jnp.logical_not(first))
            def _():
                acc[slot] += part

            @pl.when(last)
            def _():
                pltpu.make_async_copy(acc.at[slot], out.at[here], osem.at[here]).start()

        return slot

    lax.fori_loop(0, TILES, work, jnp.int32(0))

    def finish(r, c):
        pltpu.make_async_copy(zero, out.at[r], osem.at[r]).wait()
        return c

    lax.fori_loop(0, ROWS_G, finish, 0)
    token[...] = jnp.zeros_like(token)


def near_call(idx, row, col, has, tiles, side):
    smem = pl.BlockSpec(memory_space=pltpu.SMEM)
    hbm = pl.BlockSpec(memory_space=pltpu.HBM)
    return pl.pallas_call(
        near_kernel,
        out_shape=[jax.ShapeDtypeStruct((ROWS_G, EDGE, RANK), F32), jax.ShapeDtypeStruct((8, 128), F32)],
        in_specs=[smem] * 4 + [hbm] * 2,
        out_specs=[hbm, pl.BlockSpec(memory_space=pltpu.VMEM)],
        scratch_shapes=[
            pltpu.VMEM((TILES, EDGE, EDGE), BF16),
            pltpu.VMEM((TILES, EDGE, RANK), BF16),
            pltpu.VMEM((TILES, EDGE, RANK), F32),
            pltpu.VMEM((EDGE, RANK), F32),
            pltpu.SemaphoreType.DMA((TILES,)),
            pltpu.SemaphoreType.DMA((TILES,)),
            pltpu.SemaphoreType.DMA((ROWS_G,)),
        ],
        compiler_params=pltpu.CompilerParams(vmem_limit_bytes=40 * 2**20),
        name="near",
    )(idx, row, col, has, in_hbm(tiles), in_hbm(side))


def far_kernel(idx, pos, src, unit, has, tiles, *refs):
    srcs = refs[:15]
    out, tbuf, bbuf, acc, zero, tsem, bsem, osem = refs[15:]
    zero[...] = jnp.zeros_like(zero)

    def blank(r, c):
        @pl.when(has[r] == 0)
        def _():
            pltpu.make_async_copy(zero, out.at[r], osem.at[r]).start()

        return c

    def tile_copy(t, i):
        return pltpu.make_async_copy(tiles.at[i], tbuf.at[t], tsem.at[t])

    def side_copy(t, ref, u):
        return pltpu.make_async_copy(ref.at[pl.ds(u, 2)], bbuf.at[t], bsem.at[t])

    def load(t, c):
        @pl.when(pos[t] < COLS_G)
        def _():
            tile_copy(t, idx[t]).start()
            for k, ref in enumerate(srcs):
                @pl.when(src[t] == k)
                def _():
                    side_copy(t, ref, unit[t]).start()

        return c

    lax.fori_loop(0, TILES, load, 0)
    lax.fori_loop(0, COLS_G, blank, 0)

    def work(t, slot):
        here = pos[t]
        before = pos[jnp.maximum(t - 1, 0)]
        after = pos[jnp.minimum(t + 1, TILES - 1)]
        first = jnp.logical_or(t == 0, before != here)
        last = jnp.logical_or(t == TILES - 1, after != here)
        slot = jnp.where(first, t, slot)

        @pl.when(here < COLS_G)
        def _():
            tile_copy(t, 0).wait()
            side_copy(t, srcs[0], 0).wait()
            block = bbuf[t].reshape(EDGE, RANK)
            part = lax.dot_general(
                tbuf[t], block, (((0,), (0,)), ((), ())), preferred_element_type=F32
            )

            @pl.when(first)
            def _():
                acc[slot] = part

            @pl.when(jnp.logical_not(first))
            def _():
                acc[slot] += part

            @pl.when(last)
            def _():
                pltpu.make_async_copy(acc.at[slot], out.at[here], osem.at[here]).start()

        return slot

    lax.fori_loop(0, TILES, work, jnp.int32(0))

    def finish(r, c):
        pltpu.make_async_copy(zero, out.at[r], osem.at[r]).wait()
        return c

    lax.fori_loop(0, COLS_G, finish, 0)


def far_call(idx, pos, src, unit, has, tiles, srcs):
    smem = pl.BlockSpec(memory_space=pltpu.SMEM)
    anym = pl.BlockSpec(memory_space=pl.ANY)
    return pl.pallas_call(
        far_kernel,
        out_shape=jax.ShapeDtypeStruct((COLS_G, EDGE, RANK), F32),
        in_specs=[smem] * 5 + [anym] * 16,
        out_specs=anym,
        scratch_shapes=[
            pltpu.VMEM((TILES, EDGE, EDGE), BF16),
            pltpu.VMEM((TILES, 2, HALF, RANK), BF16),
            pltpu.VMEM((TILES, EDGE, RANK), F32),
            pltpu.VMEM((EDGE, RANK), F32),
            pltpu.SemaphoreType.DMA((TILES,)),
            pltpu.SemaphoreType.DMA((TILES,)),
            pltpu.SemaphoreType.DMA((COLS_G,)),
        ],
        compiler_params=pltpu.CompilerParams(vmem_limit_bytes=40 * 2**20),
        name="far",
    )(idx, pos, src, unit, has, in_hbm(tiles), *srcs)


def tdot(a, b):
    return lax.dot_general(a, b, (((0,), (0,)), ((), ())), preferred_element_type=F32, precision=HI)


def ntdot(a, b):
    return lax.dot_general(a, b, (((1,), (1,)), ((), ())), preferred_element_type=F32, precision=HI)


def hdot(a, b):
    return jnp.dot(a, b, preferred_element_type=F32, precision=HI)


def put_packed(pack, base, full):
    pack[base : base + 128, :] = full[:128, :128]
    pack[base + 128 : base + 256, :] = full[128:, :128]
    pack[base + 256 : base + 384, :] = full[128:, 128:]


def split_packed(pack, base, keep, send, at):
    place = lax.axis_index("row")
    x, core = place // CORES, place % CORES
    for s in range(XS):
        chunk = lax.rem(x + s, XS) * CHUNK
        for ref, c in ((keep, core), (send, 1 - core)):
            start = pl.multiple_of(base + c * (PACK // 2) + chunk, 8)
            ref[s, at : at + CHUNK, :] = pack[pl.ds(start, CHUNK), :]


def join_packed(pack, base, mine, other, at):
    place = lax.axis_index("row")
    x, core = place // CORES, place % CORES
    for s in range(XS):
        chunk = lax.rem(x + XS - s, XS) * CHUNK
        for ref, c in ((mine, core), (other, 1 - core)):
            start = pl.multiple_of(base + c * (PACK // 2) + chunk, 8)
            pack[pl.ds(start, CHUNK), :] = ref[s, at : at + CHUNK, :]


def take_packed(pack, base, full):
    a = pack[base : base + 128, :]
    b = pack[base + 128 : base + 256, :]
    c = pack[base + 256 : base + 384, :]
    low = lax.broadcasted_iota(jnp.int32, (128, 128), 0) >= lax.broadcasted_iota(jnp.int32, (128, 128), 1)
    full[:128, :128] = jnp.where(low, a, a.T)
    full[128:, :128] = b
    full[:128, 128:] = b.T
    full[128:, 128:] = jnp.where(low, c, c.T)


def factor64(parts, off):
    rows_in = lax.broadcasted_iota(jnp.int32, (8, 128), 0)
    parts = list(parts)
    for g in range(8):
        cols = {
            r: [jnp.broadcast_to(parts[r][:, off + 8 * g + q : off + 8 * g + q + 1], (8, 128)) for q in range(8)]
            for r in range(g, 8)
        }
        pivots = jnp.zeros((8, 128), F32)
        for q in range(8):
            pivot = jnp.broadcast_to(cols[g][q][q : q + 1, :], (8, 128))
            pivots = jnp.where(rows_in == q, pivot, pivots)
            guess = pl.reciprocal(pivot, approx=True)
            guess = guess * (2.0 - pivot * guess)
            inverse = guess * (2.0 - pivot * guess)
            line = jnp.broadcast_to(parts[g][q : q + 1, :], (8, 128)) * inverse
            heads = {w: jnp.broadcast_to(cols[g][w][q : q + 1, :], (8, 128)) for w in range(q + 1, 8)}
            for r in range(g, 8):
                factor = cols[r][q]
                if r == g:
                    factor = jnp.where(rows_in > q, factor, 0.0)
                for w in range(q + 1, 8):
                    cols[r][w] = cols[r][w] - (factor * heads[w]) * inverse
                parts[r] = parts[r] - factor * line
        parts[g] = parts[g] * lax.rsqrt(pivots)
    return parts


def factor_inverse(a_ref, w_ref):
    lanes = lax.broadcasted_iota(jnp.int32, (RANK, RANK), 1)
    rows = lax.broadcasted_iota(jnp.int32, (RANK, RANK), 0)
    w_ref[...] = jnp.where(rows == lanes, 1.0, 0.0).astype(F32)
    lane = lax.broadcasted_iota(jnp.int32, (8, 128), 1)
    row8 = lax.broadcasted_iota(jnp.int32, (8, 128), 0)
    for k in range(4):
        lo, group = 64 * k, 128 * (k // 2)
        off = 64 * (k % 2)
        eye_off = 64 - off
        in_block = jnp.logical_and(lane >= off, lane < off + 64)
        parts = []
        for r in range(8):
            piece = a_ref[lo + 8 * r : lo + 8 * r + 8, group : group + 128]
            eye = jnp.where(lane - eye_off == row8 + 8 * r, 1.0, 0.0).astype(F32)
            parts.append(jnp.where(in_block, piece, eye))
        parts = factor64(parts, off)
        kept = [jnp.where(in_block, 0.0, part) for part in parts]
        block = jnp.concatenate(kept, axis=0)
        turned = pltpu.roll(block, 64, 1)
        at_block, at_zero = (turned, turned) if off == 0 else (turned, block)
        w_here = hdot(at_zero[:, :64], w_ref[lo : lo + 64, :])
        w_ref[lo : lo + 64, :] = w_here
        if k < 3:
            start = 128 * ((k + 1) // 2)
            panel = ntdot(a_ref[start:, group : group + 128], at_block)
            a_ref[start:, start:] = a_ref[start:, start:] - ntdot(panel, panel)
            rest = lo + 64
            w_ref[rest:, :] = w_ref[rest:, :] - hdot(panel[rest - start :, :], w_here)


def near_inverse(a_ref, w_ref):
    rows = lax.broadcasted_iota(jnp.int32, (RANK, RANK), 0)
    lanes = lax.broadcasted_iota(jnp.int32, (RANK, RANK), 1)
    eye = jnp.where(rows == lanes, 1.0, 0.0).astype(F32)
    weight = jnp.where(rows > lanes, 1.0, jnp.where(rows == lanes, 0.5, 0.0)).astype(F32)
    lower = weight * (a_ref[...] - eye)
    w_ref[...] = eye - lower + hdot(lower, lower)

    def step(carry):
        count, _ = carry
        w = w_ref[...]
        rest = ntdot(hdot(w, a_ref[...]), w) - eye
        lower = weight * rest
        w_ref[...] = w - hdot(lower, w - hdot(lower, w))
        return count + 1, jnp.sum(rest * rest)

    def more(carry):
        count, size = carry
        return (count < 6) & (size > CLOSE) & (size < 16.0)

    _, size = lax.while_loop(more, step, (jnp.int32(0), F32(1.0)))
    return size


def old_gram_kernel(side, token, half, pack):
    del token
    gram = jnp.zeros((RANK, RANK), F32)
    for b in range(COLS_G):
        value = side[b]
        gram += lax.dot_general(value, value, (((0,), (0,)), ((), ())), preferred_element_type=F32)
    put_packed(pack, 0, gram)
    core = lax.rem(lax.axis_index("row"), CORES)
    half[...] = pack[pl.ds(pl.multiple_of(core * (PACK // 2), 8), PACK // 2), :]


def old_factor_kernel(mine, other, w_out, pack, a_ref, w_ref):
    core = lax.rem(lax.axis_index("row"), CORES)
    for ref, c in ((mine, core), (other, 1 - core)):
        pack[pl.ds(pl.multiple_of(c * (PACK // 2), 8), PACK // 2), :] = ref[...]
    take_packed(pack, 0, a_ref)
    factor_inverse(a_ref, w_ref)
    w_out[...] = w_ref[...] * jnp.sqrt(F32(131072.0))


def apply_kernel(row, col, old, w, prod, first, keep, send, pack):
    value = row[...].reshape(2 * EDGE, RANK) + col[...].reshape(2 * EDGE, RANK)
    prod[...] = value
    scale = jnp.sqrt(F32(131072.0))
    put_packed(pack, 0, tdot(old[...].reshape(2 * EDGE, RANK).astype(F32), value) / scale)
    split_packed(pack, 0, keep, send, CHUNK)
    better = ntdot(value, w[...])
    first[...] = better
    put_packed(pack, 0, tdot(better, better))
    split_packed(pack, 0, keep, send, 0)


def gram_kernel(prod, keep, send, pack):
    value = prod[...]
    put_packed(pack, 0, tdot(value, value))
    split_packed(pack, 0, keep, send, 0)


def pass_kernel(mine, other, value, out, pack, a_ref, w_ref):
    join_packed(pack, 0, mine, other, 0)
    take_packed(pack, 0, a_ref)
    factor_inverse(a_ref, w_ref)
    out[...] = ntdot(value[...], w_ref[...])


def diagonal_sum(value):
    spot = lax.broadcasted_iota(jnp.int32, value.shape, 0) == lax.broadcasted_iota(jnp.int32, value.shape, 1)
    return jnp.sum(jnp.where(spot, value, 0.0))


def end_kernel(mine, other, first, out, proj, flag, pack, a_ref, w_ref):
    join_packed(pack, 0, mine, other, CHUNK)
    take_packed(pack, 0, proj)
    join_packed(pack, 0, mine, other, 0)
    take_packed(pack, 0, a_ref)
    size = diagonal_sum(a_ref[...])
    mean = jnp.full((1, 1), size) / RANK
    a_ref[...] = a_ref[...] / mean
    left = near_inverse(a_ref, w_ref)
    w = w_ref[...]
    good = (left <= CLOSE) & (RANK * jnp.sum(w * w) <= BOUND) & (size > 1e-25) & (size < 1e30)
    flag[0] = good.astype(jnp.int32)
    value = ntdot(first[...], w) * jnp.sqrt(131072.0 / mean)
    out[...] = value.astype(BF16).reshape(2, EDGE, RANK)


def dense_call(kernel, outs, scratch, name, *args):
    vm = pl.BlockSpec(memory_space=pltpu.VMEM)
    return pl.pallas_call(
        kernel,
        out_shape=[jax.ShapeDtypeStruct(s, d) for s, d in outs],
        in_specs=[vm] * len(args),
        out_specs=[pl.BlockSpec(memory_space=pltpu.SMEM) if s == (1,) else vm for s, _ in outs],
        scratch_shapes=[pltpu.VMEM(s, F32) for s in scratch],
        compiler_params=pltpu.CompilerParams(vmem_limit_bytes=32 * 2**20),
        name=name,
    )(*args)


def ranked(key, *values):
    n = key.shape[0]
    where = jnp.arange(n, dtype=jnp.int32)
    before = (key[None, :] < key[:, None]) | ((key[None, :] == key[:, None]) & (where[None, :] < where[:, None]))
    rank = jnp.sum(before.astype(jnp.int32), axis=1)
    pick = rank[None, :] == where[:, None]
    return [jnp.sum(jnp.where(pick, v[None, :], 0), axis=1) for v in (key, where) + values]


def per_device(tile_list, tile_values, block_order, basis):
    row_here = lax.axis_index("row")
    col_here = lax.axis_index("col")
    x_here, core_here = row_here // 2, row_here % 2
    z_here, y_here = col_here // 4, col_here % 4

    side = lax.all_gather(basis, "row", axis=0, tiled=True)

    slot_range = jnp.arange(256, dtype=jnp.int32)
    present = tile_list[:, 0] >= 0
    match = block_order[None, None, :] == tile_list[:, :, None]
    slots = jnp.sum(jnp.where(match, slot_range[None, None, :], 0), axis=2)
    first_slot, second_slot = slots[:, 0], slots[:, 1]
    row_local = jnp.where(present, first_slot - row_here * ROWS_G, ROWS_G)
    second_owner = second_slot // 2
    second_row = second_owner // 16
    col_local = jnp.where(present, second_row * 2 + second_slot % 2, 0)
    second_x, second_core = second_row // 2, second_row % 2
    col_pos = (second_core ^ core_here) * 8 + ((second_x - x_here) % 4) * 2 + second_slot % 2
    col_pos = jnp.where(present, col_pos, COLS_G)
    n_row, n_idx, n_col = ranked(row_local, col_local)
    n_has = jnp.sum((row_local[None, :] == jnp.arange(ROWS_G)[:, None]).astype(jnp.int32), axis=1)
    f_has = jnp.sum((col_pos[None, :] == jnp.arange(COLS_G)[:, None]).astype(jnp.int32), axis=1)
    first_owner = (first_slot // 2) % 16
    dz = (first_owner // 4 - z_here) % 4
    dy = (first_owner % 4 - y_here) % 4
    odd = first_slot % 2
    outer = jnp.where(odd == 0, dz, dy)
    inner = jnp.where(odd == 0, dy, dz)
    alone = inner == 0
    six = jnp.where(inner == 3, 0, jnp.where(inner == 1, 2, 4))
    four = jnp.where((inner == 3) | (inner == 2), 2, 0)
    base = jnp.where(outer == 0, 0, jnp.where(outer == 3, 2, 4))
    kind = jnp.where(outer == 2, jnp.where((inner == 1) | (inner == 2), 7, 6), jnp.where(alone, base, base + 1))
    kind = jnp.where((kind == 0) | (odd == 0), kind, kind + 7)
    unit = jnp.where(outer == 2, four, jnp.where(alone, 2 * odd, six))
    f_pos, f_idx, f_src, f_unit = ranked(col_pos, kind, unit)

    own, groups = gather_plane(basis)
    side, groups = lax.optimization_barrier((side, groups))
    planes = finish_plane(own, groups)
    near, token = near_call(n_idx, n_row, n_col, n_has, tile_values, side)
    row_owned = lax.psum_scatter(near, "col", scatter_dimension=0, tiled=True)

    far = far_call(f_idx, f_pos, f_src, f_unit, f_has, tile_values, planes)
    far = far.reshape(2, 4, 2, EDGE, RANK)
    chip = far[0] + shift(far[1], "core")
    col_owned = jnp.concatenate(reduce4(chip[0], chip[1], chip[2], chip[3], "x"), axis=0)

    halves = [((4, CHUNK, 128), F32)] * 2
    squares = [(PACK, 128), (RANK, RANK), (RANK, RANK)]
    tall = ((2 * EDGE, RANK), F32)
    (half,) = dense_call(old_gram_kernel, [((PACK // 2, 128), F32)], [(PACK, 128)], "old_gram", side, token)
    half = exchange4(exchange4(half, "y"), "z")
    mine, other = half, shift(half, "core")
    (w,) = dense_call(old_factor_kernel, [((RANK, RANK), F32)], squares, "old_factor", mine, other)
    product, first, keep, send = dense_call(
        apply_kernel,
        [tall, tall] + [((4, 2 * CHUNK, 128), F32)] * 2,
        [(PACK, 128)],
        "apply",
        row_owned,
        col_owned,
        basis,
        w,
    )
    mine, other = reduce_all(keep, send)
    wide = ((2, EDGE, RANK), BF16)
    quick, projected, flag = dense_call(
        end_kernel, [wide, ((RANK, RANK), F32), ((1,), jnp.int32)], squares, "end", mine, other, first
    )

    def one_pass(_, value):
        keep, send = dense_call(gram_kernel, halves, [(PACK, 128)], "gram", value)
        mine, other = reduce_all(keep, send)
        return dense_call(pass_kernel, [tall], squares, "pass", mine, other, value)[0]

    def two_passes(product):
        value = lax.fori_loop(0, 2, one_pass, product)
        return (value * jnp.sqrt(F32(131072.0))).astype(BF16).reshape(2, EDGE, RANK)

    basis_out = lax.cond(flag[0] == 1, lambda p: quick, two_passes, product)
    return (basis_out, projected)


def solution(mesh):
    in_specs = (
        P(("row", "col"), None),
        P(("row", "col"), None, None),
        P(),
        P(("row", "col"), None, None),
    )
    out_specs = (P(("row", "col"), None, None), P())
    return jax.shard_map(per_device, mesh=mesh, in_specs=in_specs, out_specs=out_specs, check_vma=False)
```

```python
import jax
import jax.numpy as jnp
from jax import lax
from jax.experimental import pallas as pl
from jax.experimental.pallas import tpu as pltpu
from jax.sharding import PartitionSpec as P

HI = lax.Precision.HIGHEST
F32 = jnp.float32
BF16 = jnp.bfloat16
XS, CORES, YS, ZS = 4, 2, 4, 4
TILES = 16
ROWS_G, COLS_G = 32, 16
HALF = 256
RANK = 256
EDGE = 512
PACK = 384
CHUNK = PACK // (CORES * XS)
BOUND = 2.0**20
CLOSE = 1e-6
FLOPS = {"old_factor": 10**10, "end": 5 * 10**9, "apply": 4 * 10**9}


def ring(dim, step):
    if dim == "x":
        return "row", [(i, ((i // 2 + step) % 4) * 2 + i % 2) for i in range(8)]
    if dim == "core":
        return "row", [(i, i ^ 1) for i in range(8)]
    if dim == "y":
        return "col", [(i, (i // 4) * 4 + (i + step) % 4) for i in range(16)]
    return "col", [(i, ((i // 4 + step) % 4) * 4 + i % 4) for i in range(16)]


def shift(value, dim, step=0):
    axis, pairs = ring(dim, step)
    return lax.ppermute(value, axis, pairs)


def gather_plane(basis):
    own = basis.reshape(4, HALF, RANK)
    y_below, y_above = shift(own, "y", 1), shift(own, "y", -1)
    z_below, z_above = shift(own, "z", 1), shift(own, "z", -1)
    lines = []
    for odd, first, near in ((0, "y", (y_below, y_above)), (1, "z", (z_below, z_above))):
        lo = 2 * odd
        opposite = [shift(near[0][lo : lo + 1], first, 1), shift(near[1][lo + 1 : lo + 2], first, -1)]
        line = jnp.concatenate([near[0][lo : lo + 2], near[1][lo : lo + 2]] + opposite, axis=0)
        lines.append(line)
    groups = [
        (far, line, shift(line, second, 1), shift(line, second, -1))
        for far, line, second in zip(((z_below, z_above), (y_below, y_above)), lines, "zy")
    ]
    return own, groups


def finish_plane(own, groups):
    found = [own]
    for lo, second, (far, line, below, above) in zip((0, 2), "zy", groups):
        low = shift(jnp.concatenate([far[0][lo : lo + 2], below[:2]], axis=0), second, 1)
        high = shift(above[2:], second, -1)
        found += [line, far[0], below, far[1], above, low, high]
    return found


def reduce4(own, up, far, down, dim):
    half = own.shape[0] // 2
    relay_up = shift(far[:half], dim, 1)
    relay_down = shift(far[half:], dim, -1)
    early_up = shift(up[half:], dim, 1)
    early_down = shift(down[:half], dim, -1)
    late_up = shift(up[:half] + relay_up, dim, 1)
    late_down = shift(down[half:] + relay_down, dim, -1)
    return (own[:half] + late_up + early_down, own[half:] + early_up + late_down)


def exchange4(value, dim):
    got = [shift(value, dim, s) for s in (1, 2, 3)]
    return (value + got[1]) + (got[0] + got[2])


def reduce_all(keep, send):
    mine = keep + shift(send, "core")
    got = [shift(mine[s], "x", s) for s in (1, 2, 3)]
    value = (mine[0] + got[1]) + (got[0] + got[2])
    value = exchange4(value, "y")
    value = exchange4(value, "z")
    whole = jnp.stack([value] + [shift(value, "x", s) for s in (1, 2, 3)])
    return whole, shift(whole, "core")


def in_hbm(value):
    return pltpu.with_memory_space_constraint(value, pltpu.HBM)


def near_kernel(idx, row, col, has, tiles, side, out, token, tbuf, bbuf, acc, zero, tsem, bsem, osem):
    zero[...] = jnp.zeros_like(zero)

    def blank(r, c):
        @pl.when(has[r] == 0)
        def _():
            pltpu.make_async_copy(zero, out.at[r], osem.at[r]).start()

        return c

    def tile_copy(t, i):
        return pltpu.make_async_copy(tiles.at[i], tbuf.at[t], tsem.at[t])

    def side_copy(t, b):
        return pltpu.make_async_copy(side.at[b], bbuf.at[t], bsem.at[t])

    def load(t, c):
        @pl.when(row[t] < ROWS_G)
        def _():
            tile_copy(t, idx[t]).start()
            side_copy(t, col[t]).start()

        return c

    lax.fori_loop(0, TILES, load, 0)
    lax.fori_loop(0, ROWS_G, blank, 0)

    def work(t, slot):
        here = row[t]
        before = row[jnp.maximum(t - 1, 0)]
        after = row[jnp.minimum(t + 1, TILES - 1)]
        first = jnp.logical_or(t == 0, before != here)
        last = jnp.logical_or(t == TILES - 1, after != here)
        slot = jnp.where(first, t, slot)

        @pl.when(here < ROWS_G)
        def _():
            tile_copy(t, 0).wait()
            side_copy(t, 0).wait()
            part = jnp.dot(tbuf[t], bbuf[t], preferred_element_type=F32)

            @pl.when(first)
            def _():
                acc[slot] = part

            @pl.when(jnp.logical_not(first))
            def _():
                acc[slot] += part

            @pl.when(last)
            def _():
                pltpu.make_async_copy(acc.at[slot], out.at[here], osem.at[here]).start()

        return slot

    lax.fori_loop(0, TILES, work, jnp.int32(0))

    def finish(r, c):
        pltpu.make_async_copy(zero, out.at[r], osem.at[r]).wait()
        return c

    lax.fori_loop(0, ROWS_G, finish, 0)
    token[...] = jnp.zeros_like(token)


def near_call(idx, row, col, has, tiles, side):
    smem = pl.BlockSpec(memory_space=pltpu.SMEM)
    hbm = pl.BlockSpec(memory_space=pltpu.HBM)
    return pl.pallas_call(
        near_kernel,
        out_shape=[jax.ShapeDtypeStruct((ROWS_G, EDGE, RANK), F32), jax.ShapeDtypeStruct((8, 128), F32)],
        in_specs=[smem] * 4 + [hbm] * 2,
        out_specs=[hbm, pl.BlockSpec(memory_space=pltpu.VMEM)],
        scratch_shapes=[
            pltpu.VMEM((TILES, EDGE, EDGE), BF16),
            pltpu.VMEM((TILES, EDGE, RANK), BF16),
            pltpu.VMEM((TILES, EDGE, RANK), F32),
            pltpu.VMEM((EDGE, RANK), F32),
            pltpu.SemaphoreType.DMA((TILES,)),
            pltpu.SemaphoreType.DMA((TILES,)),
            pltpu.SemaphoreType.DMA((ROWS_G,)),
        ],
        compiler_params=pltpu.CompilerParams(vmem_limit_bytes=40 * 2**20),
        cost_estimate=pl.CostEstimate(flops=TILES * 2 * EDGE * EDGE * RANK, bytes_accessed=32 * 2**20, transcendentals=0),
        name="near",
    )(idx, row, col, has, in_hbm(tiles), in_hbm(side))


def far_kernel(idx, pos, src, unit, has, tiles, *refs):
    srcs = refs[:15]
    out, tbuf, bbuf, acc, zero, tsem, bsem, osem = refs[15:]
    zero[...] = jnp.zeros_like(zero)

    def blank(r, c):
        @pl.when(has[r] == 0)
        def _():
            pltpu.make_async_copy(zero, out.at[r], osem.at[r]).start()

        return c

    def tile_copy(t, i):
        return pltpu.make_async_copy(tiles.at[i], tbuf.at[t], tsem.at[t])

    def side_copy(t, ref, u):
        return pltpu.make_async_copy(ref.at[pl.ds(u, 2)], bbuf.at[t], bsem.at[t])

    def load(t, c):
        @pl.when(pos[t] < COLS_G)
        def _():
            tile_copy(t, idx[t]).start()
            for k, ref in enumerate(srcs):
                @pl.when(src[t] == k)
                def _():
                    side_copy(t, ref, unit[t]).start()

        return c

    lax.fori_loop(0, TILES, load, 0)
    lax.fori_loop(0, COLS_G, blank, 0)

    def work(t, slot):
        here = pos[t]
        before = pos[jnp.maximum(t - 1, 0)]
        after = pos[jnp.minimum(t + 1, TILES - 1)]
        first = jnp.logical_or(t == 0, before != here)
        last = jnp.logical_or(t == TILES - 1, after != here)
        slot = jnp.where(first, t, slot)

        @pl.when(here < COLS_G)
        def _():
            tile_copy(t, 0).wait()
            side_copy(t, srcs[0], 0).wait()
            block = bbuf[t].reshape(EDGE, RANK)
            part = lax.dot_general(
                tbuf[t], block, (((0,), (0,)), ((), ())), preferred_element_type=F32
            )

            @pl.when(first)
            def _():
                acc[slot] = part

            @pl.when(jnp.logical_not(first))
            def _():
                acc[slot] += part

            @pl.when(last)
            def _():
                pltpu.make_async_copy(acc.at[slot], out.at[here], osem.at[here]).start()

        return slot

    lax.fori_loop(0, TILES, work, jnp.int32(0))

    def finish(r, c):
        pltpu.make_async_copy(zero, out.at[r], osem.at[r]).wait()
        return c

    lax.fori_loop(0, COLS_G, finish, 0)


def far_call(idx, pos, src, unit, has, tiles, srcs):
    smem = pl.BlockSpec(memory_space=pltpu.SMEM)
    anym = pl.BlockSpec(memory_space=pl.ANY)
    return pl.pallas_call(
        far_kernel,
        out_shape=jax.ShapeDtypeStruct((COLS_G, EDGE, RANK), F32),
        in_specs=[smem] * 5 + [anym] * 16,
        out_specs=anym,
        scratch_shapes=[
            pltpu.VMEM((TILES, EDGE, EDGE), BF16),
            pltpu.VMEM((TILES, 2, HALF, RANK), BF16),
            pltpu.VMEM((TILES, EDGE, RANK), F32),
            pltpu.VMEM((EDGE, RANK), F32),
            pltpu.SemaphoreType.DMA((TILES,)),
            pltpu.SemaphoreType.DMA((TILES,)),
            pltpu.SemaphoreType.DMA((COLS_G,)),
        ],
        compiler_params=pltpu.CompilerParams(vmem_limit_bytes=40 * 2**20),
        cost_estimate=pl.CostEstimate(flops=TILES * 2 * EDGE * EDGE * RANK, bytes_accessed=24 * 2**20, transcendentals=0),
        name="far",
    )(idx, pos, src, unit, has, in_hbm(tiles), *srcs)


def tdot(a, b):
    return lax.dot_general(a, b, (((0,), (0,)), ((), ())), preferred_element_type=F32, precision=HI)


def ntdot(a, b):
    return lax.dot_general(a, b, (((1,), (1,)), ((), ())), preferred_element_type=F32, precision=HI)


def hdot(a, b):
    return jnp.dot(a, b, preferred_element_type=F32, precision=HI)


def put_packed(pack, base, full):
    pack[base : base + 128, :] = full[:128, :128]
    pack[base + 128 : base + 256, :] = full[128:, :128]
    pack[base + 256 : base + 384, :] = full[128:, 128:]


def split_packed(pack, base, keep, send, at):
    place = lax.axis_index("row")
    x, core = place // CORES, place % CORES
    for s in range(XS):
        chunk = lax.rem(x + s, XS) * CHUNK
        for ref, c in ((keep, core), (send, 1 - core)):
            start = pl.multiple_of(base + c * (PACK // 2) + chunk, 8)
            ref[s, at : at + CHUNK, :] = pack[pl.ds(start, CHUNK), :]


def join_packed(pack, base, mine, other, at):
    place = lax.axis_index("row")
    x, core = place // CORES, place % CORES
    for s in range(XS):
        chunk = lax.rem(x + XS - s, XS) * CHUNK
        for ref, c in ((mine, core), (other, 1 - core)):
            start = pl.multiple_of(base + c * (PACK // 2) + chunk, 8)
            pack[pl.ds(start, CHUNK), :] = ref[s, at : at + CHUNK, :]


def take_packed(pack, base, full):
    a = pack[base : base + 128, :]
    b = pack[base + 128 : base + 256, :]
    c = pack[base + 256 : base + 384, :]
    low = lax.broadcasted_iota(jnp.int32, (128, 128), 0) >= lax.broadcasted_iota(jnp.int32, (128, 128), 1)
    full[:128, :128] = jnp.where(low, a, a.T)
    full[128:, :128] = b
    full[:128, 128:] = b.T
    full[128:, 128:] = jnp.where(low, c, c.T)


def factor64(parts, off):
    rows_in = lax.broadcasted_iota(jnp.int32, (8, 128), 0)
    parts = list(parts)
    for g in range(8):
        cols = {
            r: [jnp.broadcast_to(parts[r][:, off + 8 * g + q : off + 8 * g + q + 1], (8, 128)) for q in range(8)]
            for r in range(g, 8)
        }
        pivots = jnp.zeros((8, 128), F32)
        for q in range(8):
            pivot = jnp.broadcast_to(cols[g][q][q : q + 1, :], (8, 128))
            pivots = jnp.where(rows_in == q, pivot, pivots)
            guess = pl.reciprocal(pivot, approx=True)
            guess = guess * (2.0 - pivot * guess)
            inverse = guess * (2.0 - pivot * guess)
            line = jnp.broadcast_to(parts[g][q : q + 1, :], (8, 128)) * inverse
            heads = {w: jnp.broadcast_to(cols[g][w][q : q + 1, :], (8, 128)) for w in range(q + 1, 8)}
            for r in range(g, 8):
                factor = cols[r][q]
                if r == g:
                    factor = jnp.where(rows_in > q, factor, 0.0)
                for w in range(q + 1, 8):
                    cols[r][w] = cols[r][w] - (factor * heads[w]) * inverse
                parts[r] = parts[r] - factor * line
        parts[g] = parts[g] * lax.rsqrt(pivots)
    return parts


def factor_inverse(a_ref, w_ref):
    lanes = lax.broadcasted_iota(jnp.int32, (RANK, RANK), 1)
    rows = lax.broadcasted_iota(jnp.int32, (RANK, RANK), 0)
    w_ref[...] = jnp.where(rows == lanes, 1.0, 0.0).astype(F32)
    lane = lax.broadcasted_iota(jnp.int32, (8, 128), 1)
    row8 = lax.broadcasted_iota(jnp.int32, (8, 128), 0)
    for k in range(4):
        lo, group = 64 * k, 128 * (k // 2)
        off = 64 * (k % 2)
        eye_off = 64 - off
        in_block = jnp.logical_and(lane >= off, lane < off + 64)
        parts = []
        for r in range(8):
            piece = a_ref[lo + 8 * r : lo + 8 * r + 8, group : group + 128]
            eye = jnp.where(lane - eye_off == row8 + 8 * r, 1.0, 0.0).astype(F32)
            parts.append(jnp.where(in_block, piece, eye))
        parts = factor64(parts, off)
        kept = [jnp.where(in_block, 0.0, part) for part in parts]
        block = jnp.concatenate(kept, axis=0)
        turned = pltpu.roll(block, 64, 1)
        at_block, at_zero = (turned, turned) if off == 0 else (turned, block)
        w_here = hdot(at_zero[:, :64], w_ref[lo : lo + 64, :])
        w_ref[lo : lo + 64, :] = w_here
        if k < 3:
            start = 128 * ((k + 1) // 2)
            panel = ntdot(a_ref[start:, group : group + 128], at_block)
            a_ref[start:, start:] = a_ref[start:, start:] - ntdot(panel, panel)
            rest = lo + 64
            w_ref[rest:, :] = w_ref[rest:, :] - hdot(panel[rest - start :, :], w_here)


def near_inverse(a_ref, w_ref):
    rows = lax.broadcasted_iota(jnp.int32, (RANK, RANK), 0)
    lanes = lax.broadcasted_iota(jnp.int32, (RANK, RANK), 1)
    eye = jnp.where(rows == lanes, 1.0, 0.0).astype(F32)
    weight = jnp.where(rows > lanes, 1.0, jnp.where(rows == lanes, 0.5, 0.0)).astype(F32)
    lower = weight * (a_ref[...] - eye)
    w_ref[...] = eye - lower + hdot(lower, lower)

    def step(carry):
        count, _ = carry
        w = w_ref[...]
        rest = ntdot(hdot(w, a_ref[...]), w) - eye
        lower = weight * rest
        w_ref[...] = w - hdot(lower, w - hdot(lower, w))
        return count + 1, jnp.sum(rest * rest)

    def more(carry):
        count, size = carry
        return (count < 6) & (size > CLOSE) & (size < 16.0)

    _, size = lax.while_loop(more, step, (jnp.int32(0), F32(1.0)))
    return size


def old_gram_kernel(side, token, half, pack):
    del token
    gram = jnp.zeros((RANK, RANK), F32)
    for b in range(COLS_G):
        value = side[b]
        gram += lax.dot_general(value, value, (((0,), (0,)), ((), ())), preferred_element_type=F32)
    put_packed(pack, 0, gram)
    core = lax.rem(lax.axis_index("row"), CORES)
    half[...] = pack[pl.ds(pl.multiple_of(core * (PACK // 2), 8), PACK // 2), :]


def old_factor_kernel(mine, other, w_out, pack, a_ref, w_ref):
    core = lax.rem(lax.axis_index("row"), CORES)
    for ref, c in ((mine, core), (other, 1 - core)):
        pack[pl.ds(pl.multiple_of(c * (PACK // 2), 8), PACK // 2), :] = ref[...]
    take_packed(pack, 0, a_ref)
    factor_inverse(a_ref, w_ref)
    w_out[...] = w_ref[...] * jnp.sqrt(F32(131072.0))


def apply_kernel(row, col, old, w, prod, first, keep, send, pack):
    value = row[...].reshape(2 * EDGE, RANK) + col[...].reshape(2 * EDGE, RANK)
    prod[...] = value
    scale = jnp.sqrt(F32(131072.0))
    put_packed(pack, 0, tdot(old[...].reshape(2 * EDGE, RANK).astype(F32), value) / scale)
    split_packed(pack, 0, keep, send, CHUNK)
    better = ntdot(value, w[...])
    first[...] = better
    put_packed(pack, 0, tdot(better, better))
    split_packed(pack, 0, keep, send, 0)


def gram_kernel(prod, keep, send, pack):
    value = prod[...]
    put_packed(pack, 0, tdot(value, value))
    split_packed(pack, 0, keep, send, 0)


def pass_kernel(mine, other, value, out, pack, a_ref, w_ref):
    join_packed(pack, 0, mine, other, 0)
    take_packed(pack, 0, a_ref)
    factor_inverse(a_ref, w_ref)
    out[...] = ntdot(value[...], w_ref[...])


def diagonal_sum(value):
    spot = lax.broadcasted_iota(jnp.int32, value.shape, 0) == lax.broadcasted_iota(jnp.int32, value.shape, 1)
    return jnp.sum(jnp.where(spot, value, 0.0))


def end_kernel(mine, other, first, out, proj, flag, pack, a_ref, w_ref):
    join_packed(pack, 0, mine, other, CHUNK)
    take_packed(pack, 0, proj)
    join_packed(pack, 0, mine, other, 0)
    take_packed(pack, 0, a_ref)
    size = diagonal_sum(a_ref[...])
    mean = jnp.full((1, 1), size) / RANK
    a_ref[...] = a_ref[...] / mean
    left = near_inverse(a_ref, w_ref)
    w = w_ref[...]
    good = (left <= CLOSE) & (RANK * jnp.sum(w * w) <= BOUND) & (size > 1e-25) & (size < 1e30)
    flag[0] = good.astype(jnp.int32)
    value = ntdot(first[...], w) * jnp.sqrt(131072.0 / mean)
    out[...] = value.astype(BF16).reshape(2, EDGE, RANK)


def dense_call(kernel, outs, scratch, name, *args):
    vm = pl.BlockSpec(memory_space=pltpu.VMEM)
    return pl.pallas_call(
        kernel,
        out_shape=[jax.ShapeDtypeStruct(s, d) for s, d in outs],
        in_specs=[vm] * len(args),
        out_specs=[pl.BlockSpec(memory_space=pltpu.SMEM) if s == (1,) else vm for s, _ in outs],
        scratch_shapes=[pltpu.VMEM(s, F32) for s in scratch],
        compiler_params=pltpu.CompilerParams(vmem_limit_bytes=32 * 2**20),
        cost_estimate=pl.CostEstimate(flops=FLOPS.get(name, 2**30), bytes_accessed=2**20, transcendentals=RANK),
        name=name,
    )(*args)


def ranked(key, *values):
    n = key.shape[0]
    where = jnp.arange(n, dtype=jnp.int32)
    before = (key[None, :] < key[:, None]) | ((key[None, :] == key[:, None]) & (where[None, :] < where[:, None]))
    rank = jnp.sum(before.astype(jnp.int32), axis=1)
    pick = rank[None, :] == where[:, None]
    return [jnp.sum(jnp.where(pick, v[None, :], 0), axis=1) for v in (key, where) + values]


def per_device(tile_list, tile_values, block_order, basis):
    row_here = lax.axis_index("row")
    col_here = lax.axis_index("col")
    x_here, core_here = row_here // 2, row_here % 2
    z_here, y_here = col_here // 4, col_here % 4

    side = lax.all_gather(basis, "row", axis=0, tiled=True)

    slot_range = jnp.arange(256, dtype=jnp.int32)
    present = tile_list[:, 0] >= 0
    match = block_order[None, None, :] == tile_list[:, :, None]
    slots = jnp.sum(jnp.where(match, slot_range[None, None, :], 0), axis=2)
    first_slot, second_slot = slots[:, 0], slots[:, 1]
    row_local = jnp.where(present, first_slot - row_here * ROWS_G, ROWS_G)
    second_owner = second_slot // 2
    second_row = second_owner // 16
    col_local = jnp.where(present, second_row * 2 + second_slot % 2, 0)
    second_x, second_core = second_row // 2, second_row % 2
    col_pos = (second_core ^ core_here) * 8 + ((second_x - x_here) % 4) * 2 + second_slot % 2
    col_pos = jnp.where(present, col_pos, COLS_G)
    n_row, n_idx, n_col = ranked(row_local, col_local)
    n_has = jnp.sum((row_local[None, :] == jnp.arange(ROWS_G)[:, None]).astype(jnp.int32), axis=1)
    f_has = jnp.sum((col_pos[None, :] == jnp.arange(COLS_G)[:, None]).astype(jnp.int32), axis=1)
    first_owner = (first_slot // 2) % 16
    dz = (first_owner // 4 - z_here) % 4
    dy = (first_owner % 4 - y_here) % 4
    odd = first_slot % 2
    outer = jnp.where(odd == 0, dz, dy)
    inner = jnp.where(odd == 0, dy, dz)
    alone = inner == 0
    six = jnp.where(inner == 3, 0, jnp.where(inner == 1, 2, 4))
    four = jnp.where((inner == 3) | (inner == 2), 2, 0)
    base = jnp.where(outer == 0, 0, jnp.where(outer == 3, 2, 4))
    kind = jnp.where(outer == 2, jnp.where((inner == 1) | (inner == 2), 7, 6), jnp.where(alone, base, base + 1))
    kind = jnp.where((kind == 0) | (odd == 0), kind, kind + 7)
    unit = jnp.where(outer == 2, four, jnp.where(alone, 2 * odd, six))
    f_pos, f_idx, f_src, f_unit = ranked(col_pos, kind, unit)

    own, groups = gather_plane(basis)
    side, groups = lax.optimization_barrier((side, groups))
    planes = finish_plane(own, groups)
    near, token = near_call(n_idx, n_row, n_col, n_has, tile_values, side)
    near, planes = lax.optimization_barrier((near, planes))
    row_owned = lax.psum_scatter(near, "col", scatter_dimension=0, tiled=True)

    far = far_call(f_idx, f_pos, f_src, f_unit, f_has, tile_values, planes)
    far = far.reshape(2, 4, 2, EDGE, RANK)
    chip = far[0] + shift(far[1], "core")
    col_owned = jnp.concatenate(reduce4(chip[0], chip[1], chip[2], chip[3], "x"), axis=0)

    halves = [((4, CHUNK, 128), F32)] * 2
    squares = [(PACK, 128), (RANK, RANK), (RANK, RANK)]
    tall = ((2 * EDGE, RANK), F32)
    (half,) = dense_call(old_gram_kernel, [((PACK // 2, 128), F32)], [(PACK, 128)], "old_gram", side, token)
    half = exchange4(exchange4(half, "y"), "z")
    mine, other = half, shift(half, "core")
    (w,) = dense_call(old_factor_kernel, [((RANK, RANK), F32)], squares, "old_factor", mine, other)
    product, first, keep, send = dense_call(
        apply_kernel,
        [tall, tall] + [((4, 2 * CHUNK, 128), F32)] * 2,
        [(PACK, 128)],
        "apply",
        row_owned,
        col_owned,
        basis,
        w,
    )
    mine, other = reduce_all(keep, send)
    wide = ((2, EDGE, RANK), BF16)
    quick, projected, flag = dense_call(
        end_kernel, [wide, ((RANK, RANK), F32), ((1,), jnp.int32)], squares, "end", mine, other, first
    )

    def one_pass(_, value):
        keep, send = dense_call(gram_kernel, halves, [(PACK, 128)], "gram", value)
        mine, other = reduce_all(keep, send)
        return dense_call(pass_kernel, [tall], squares, "pass", mine, other, value)[0]

    def two_passes(product):
        value = lax.fori_loop(0, 2, one_pass, product)
        return (value * jnp.sqrt(F32(131072.0))).astype(BF16).reshape(2, EDGE, RANK)

    basis_out = lax.cond(flag[0] == 1, lambda p: quick, two_passes, product)
    return (basis_out, projected)


def solution(mesh):
    in_specs = (
        P(("row", "col"), None),
        P(("row", "col"), None, None),
        P(),
        P(("row", "col"), None, None),
    )
    out_specs = (P(("row", "col"), None, None), P())
    return jax.shard_map(per_device, mesh=mesh, in_specs=in_specs, out_specs=out_specs, check_vma=False)
```
